32 devices in a mesh: gx: 4 (over y, core), gy: 4 (over z), sa: 2 (over x).
Axes of the slice: x: 2, y: 2, z: 4, core: 2. Of those that a mesh axis runs over, the one named last changes fastest.
Arguments:
- fields: float32 [2, 7, 16, 32, 512], P('sa', None, 'gx', 'gy'), may hold values from -6 to 6
- sources: float32 [2, 7, 16, 32, 512], P('sa', None, 'gx', 'gy'), may hold values from -5 to 5
- diagonal: float32 [7, 16, 32, 512], P(None, 'gx', 'gy'), may hold values from 0.25 to 2
- block_inverse: float32 [7, 7, 16, 32, 512], P(None, None, 'gx', 'gy'), may hold values from -0.035 to 0.14
- coupling: float32 [7], replicated, may hold values from 0.25 to 0.75
- donors: int32 [16, 3], replicated, may hold values from 0 to 895, as said below
- returns: int32 [4, 896], P('gy'), may hold values from 0 to 15
Outputs:
- fields_out: float32 [2, 7, 16, 32, 512], P('sa', None, 'gx', 'gy')
The draws below stay inside these ranges and needn't reach their ends.
Inputs may be any that keep to these rules, and one draw needn't show every extreme that they name: `donors`: column 0 is a gy position, column 1 a block index on that position's exit face, column 2 the inflow slot filled; column 2 is a permutation of 0 to 15.
All inputs are finite; a program needn't handle non-finite values.
Results may differ from the reference program's by a relative error of at most 0.00002.
Values sent between devices are 32-bit elements; how exact they have to be, the bound alone decides.
A program may use at most 128 MiB of HBM per device.

```python
import math
import jax
import jax.numpy as jnp

STATES = 7
SWEEPS = 4
BLK = 32
CX = 4
CY = 8
NX = 16
NY = 32
NZ = 512
SLOTS = 1
EXIT_FACE_BLOCKS = 896
INFLOW_SLOTS = 16
N_GX = 4
N_GY = 4


def draw_donors(key, part):
    key = jax.random.fold_in(key, 5)
    key_source, key_block, key_target = jax.random.split(key, 3)
    slot_total = N_GX * N_GY * SLOTS
    anchor = jax.random.randint(key_source, (slot_total,), 0, N_GY, dtype=jnp.int32)
    blocks = jax.random.randint(key_block, (slot_total,), 0, EXIT_FACE_BLOCKS, dtype=jnp.int32).at[0].set(EXIT_FACE_BLOCKS - 1)
    targets = jax.random.permutation(key_target, slot_total).astype(jnp.int32)
    return jnp.stack([anchor, blocks, targets], axis=1).astype(jnp.int32)


def draw_block_inverse(key, part):
    key = jax.random.fold_in(key, 7)
    diagonal_key, key_off = jax.random.split(key)
    full_shape = (STATES, STATES, NX, NY, NZ)
    identity = jnp.eye(STATES, dtype=jnp.float32)[:, :, None, None, None]
    leading = jax.random.uniform(diagonal_key, full_shape, jnp.float32, 0.1, 0.14)
    coupled = jnp.clip(0.012 * jax.random.normal(key_off, full_shape, jnp.float32), -0.035, 0.035)
    return identity * leading + (1.0 - identity) * coupled


def draw_sources(key, part):
    key = jax.random.fold_in(key, 9)
    full_shape = (2, STATES, NX, NY, NZ)
    return jnp.clip(jax.random.normal(key, full_shape, jnp.float32), -5.0, 5.0)


def place_ends(values, stream_key, low, top_value):
    shape = values.shape
    place = [jax.random.randint(jax.random.fold_in(stream_key, axis), (), 0, shape[axis]) for axis in range(len(shape))]
    values = values.at[tuple(place)].set(low)
    longest = shape.index(max(shape))
    place[longest] = (place[longest] + 1) % shape[longest]
    return values.at[tuple(place)].set(top_value)


def block_levels(key, shape, cuts, low, high):
    level = 1.0
    for position, parts in cuts:
        steps = jax.random.uniform(jax.random.fold_in(jax.random.fold_in(key, 6), position), (parts,), jnp.float32, low / len(cuts), high / len(cuts))
        level = level * jnp.repeat(jnp.exp(steps), shape[position] // parts).reshape((-1,) + (1,) * (len(shape) - 1 - position))
    return level


def noise(key, shape, width, most, cuts=(), kind=jnp.bfloat16):
    entries = jax.random.normal(key, shape, jnp.float32) * width
    if len(cuts) > 0:
        entries = block_levels(key, shape, cuts, -0.22, 0.18) * entries
    return jnp.clip(entries, min=-most, max=most).astype(kind)


def setup_inputs(seed: int = 0) -> dict:
    streams_of = jax.random.split(jax.random.key(seed), 8)
    fields = noise(streams_of[0], (2, STATES, NX, NY, NZ), 1.0, 6.0, ((0, 2), (2, 4), (3, 4)), jnp.float32)
    sources = draw_sources(jax.random.fold_in(streams_of[7], 71), 0)
    diagonal = jnp.clip(0.25 + 1.75 * jax.random.uniform(streams_of[2], (STATES, NX, NY, NZ), jnp.float32) ** block_levels(streams_of[2], (STATES, NX, NY, NZ), ((1, 4), (2, 4)), -0.2, 0.2), 0.25, 2.0)
    block_inverse = draw_block_inverse(jax.random.fold_in(streams_of[7], 71), 0)
    coupling = jnp.clip(jnp.exp(jax.random.uniform(streams_of[4], (STATES,), jnp.float32, math.log(0.25), math.log(0.75))), 0.25, 0.75)
    donors = draw_donors(jax.random.fold_in(streams_of[7], 71), 0)
    returns = place_ends(jax.random.randint(streams_of[6], (N_GY, EXIT_FACE_BLOCKS), 0, INFLOW_SLOTS), jax.random.fold_in(streams_of[6], 1), 0, INFLOW_SLOTS - 1).astype(jnp.int32)
    return dict(fields=fields, sources=sources, diagonal=diagonal, block_inverse=block_inverse, coupling=coupling, donors=donors, returns=returns)


def z_terms_combustor(values):
    blank_cap = jnp.zeros_like(values[:1, :, :, :1])
    upper_cap = jnp.concatenate([values[1:, :, :, :1], blank_cap], axis=0)
    lower_cap = jnp.concatenate([blank_cap, values[:-1, :, :, -1:]], axis=0)
    upper_terms = jnp.concatenate([values[:, :, :, 1:], upper_cap], axis=3)
    lower_terms = jnp.concatenate([lower_cap, values[:, :, :, :-1]], axis=3)
    return upper_terms, lower_terms


def z_terms_turbine(values, inflow):
    upper_cap = jnp.zeros_like(values[:, :, :, :1])
    lower_cap = jnp.concatenate([inflow[None, :, :, None], values[1:, :, :, :1]], axis=0)
    upper_terms = jnp.concatenate([values[:, :, :, 1:], upper_cap], axis=3)
    lower_terms = jnp.concatenate([lower_cap, values[:, :, :, :-1]], axis=3)
    return upper_terms, lower_terms


def neighbour_sum(padded, upper_terms, lower_terms):
    summed = padded[:, 2:, 1:-1] + padded[:, :-2, 1:-1]
    summed = summed + padded[:, 1:-1, 2:] + padded[:, 1:-1, :-2]
    return summed + upper_terms + lower_terms


def apply_inverse(block_inverse, driving):
    result = block_inverse[:, 0] * driving[0]
    for column in range(1, driving.shape[0]):
        result = result + block_inverse[:, column] * driving[column]
    return result


def reference(fields, sources, diagonal, block_inverse, coupling, donors, returns):
    combustor = fields[0]
    turbine = fields[1]
    slot_total = N_GX * N_GY * SLOTS
    inlet_blocks = turbine[0, :, :, 0].reshape(N_GX, CX, N_GY, CY).transpose(0, 2, 1, 3).reshape(slot_total, BLK)
    exit_blocks = combustor[:, NX - 1].reshape(STATES, N_GY, CY, NZ).transpose(1, 0, 2, 3).reshape(N_GY, EXIT_FACE_BLOCKS, BLK)
    filled = jnp.zeros((slot_total, BLK), jnp.float32).at[donors[:, 2]].set(exit_blocks[donors[:, 0], donors[:, 1]])
    inflow = filled.reshape(N_GX, N_GY, CX, CY).transpose(0, 2, 1, 3).reshape(NX, NY)
    pressure_back = inlet_blocks[returns].reshape(N_GY, STATES, CY, NZ).transpose(1, 0, 2, 3).reshape(STATES, NY, NZ)
    parity = (jnp.arange(NX)[:, None, None] + jnp.arange(NY)[None, :, None] + jnp.arange(NZ)[None, None, :]) % 2
    divisor = 6.0 + diagonal
    weights = coupling[:, None, None, None]
    widths = ((0, 0), (1, 1), (1, 1), (0, 0))
    for sweep_index in range(SWEEPS):
        for colour in (0, 1):
            padded = jnp.pad(combustor, widths)
            padded = padded.at[:, -1, 1:-1, :].set(pressure_back)
            upper_terms, lower_terms = z_terms_combustor(combustor)
            updated = (sources[0] + neighbour_sum(padded, upper_terms, lower_terms)) / divisor
            combustor = jnp.where(parity == colour, updated, combustor)
            padded = jnp.pad(turbine, widths)
            upper_terms, lower_terms = z_terms_turbine(turbine, inflow)
            driving = sources[1] + weights * neighbour_sum(padded, upper_terms, lower_terms)
            updated = apply_inverse(block_inverse, driving)
            turbine = jnp.where(parity == colour, updated, turbine)
    return jnp.stack([combustor, turbine])
```

```python
import functools

import jax
import jax.numpy as jnp
from jax import lax
from jax.experimental import pallas as pl
from jax.experimental.pallas import tpu as pltpu
from jax.sharding import PartitionSpec as P

SWEEPS = 4
BLK = 32
LANES = 128
MESH = pl.DeviceIdType.MESH


def kernel(
    n_gx, n_gy, sizes,
    fields, sources, diagonal, inverse, coupling, donors, returns, out,
    raw, raw_source, raw_diagonal, raw_inverse, held, source, scale, matrix, part,
    halo_x, halo_y, edge_y, inflow, wanted, table, rows, inlet, arrived,
    local_sem, send_sem, recv_sem, slot_sem, interface_sem,
):
    states, cells_x, cells_y, cells_z = sizes
    pairs = cells_x // 2
    halves = 2 * SWEEPS
    slots = n_gx * n_gy
    per_row = cells_z // BLK
    gx, gy, sa = lax.axis_index("gx"), lax.axis_index("gy"), lax.axis_index("sa")
    own = gx * n_gy + gy
    has = (
        (gx + n_gx - 1) // n_gx,
        1 - (gx + 1) // n_gx,
        (gy + n_gy - 1) // n_gy,
        1 - (gy + 1) // n_gy,
    )
    peers = ({"gx": gx - 1}, {"gx": gx + 1}, {"gy": gy - 1}, {"gy": gy + 1})
    combustor = sa == 0
    turbine = sa == 1
    at_exit = combustor & (gx == n_gx - 1)

    load_fields = pltpu.make_async_copy(fields.at[0], raw, local_sem.at[0])
    load_source = pltpu.make_async_copy(sources.at[0], raw_source, local_sem.at[1])
    load_diagonal = pltpu.make_async_copy(diagonal, raw_diagonal, local_sem.at[2])
    load_inverse = pltpu.make_async_copy(inverse, raw_inverse, local_sem.at[3])
    load_fields.start()
    load_source.start()
    pl.when(combustor)(load_diagonal.start)
    pl.when(turbine)(load_inverse.start)

    barrier = pltpu.get_barrier_semaphore()

    def greet(peer):
        pl.semaphore_signal(barrier, inc=1, device_id=peer, device_id_type=MESH)

    for there, peer in zip(has, peers):
        pl.when(there == 1)(functools.partial(greet, peer))

    @pl.when(turbine)
    def _():
        for j in range(n_gy):
            greet({"gx": n_gx - 1, "gy": j, "sa": 0})

    @pl.when(at_exit)
    def _():
        for g in range(slots):
            greet({"gx": g // n_gy, "gy": g % n_gy, "sa": 1})

    sub = lax.broadcasted_iota(jnp.int32, (cells_y, LANES), 0)
    lane = lax.broadcasted_iota(jnp.int32, (cells_y, LANES), 1)
    tall = lax.broadcasted_iota(jnp.int32, (cells_y, cells_z), 0)
    wide = lax.broadcasted_iota(jnp.int32, (cells_y, cells_z), 1)
    parity = (tall + wide) % 2
    even = parity == 0
    even_lanes = (sub + lane) % 2 == 0

    def split(even_plane, odd_plane):
        return (jnp.where(even, even_plane, odd_plane), jnp.where(even, odd_plane, even_plane))

    def stage_y(colour):
        for p in range(pairs):
            for k in range(states):
                edge_y[0, colour, p, k] = held[colour, p, k, 0:1, :]
                edge_y[1, colour, p, k] = held[colour, p, k, cells_y - 1 : cells_y, :]

    def halo_copy(way, colour, half):
        if way == 0:
            ends = (held.at[colour, 0], halo_x.at[1, half])
        elif way == 1:
            ends = (held.at[colour, pairs - 1], halo_x.at[0, half])
        else:
            ends = (edge_y.at[way - 2, colour], halo_y.at[3 - way, half])
        return pltpu.make_async_remote_copy(
            src_ref=ends[0],
            dst_ref=ends[1],
            send_sem=send_sem.at[way, half],
            recv_sem=recv_sem.at[way, half],
            device_id=peers[way],
            device_id_type=MESH,
        )

    def send(ways, colour, half):
        for way in ways:
            pl.when(has[way] == 1)(lambda way=way: halo_copy(way, colour, half).start())

    def wait_sent(colour, half):
        for way in range(4):
            pl.when(has[way] == 1)(lambda way=way: halo_copy(way, colour, half).wait_send())

    def wait_received(colour, half):
        for way in range(4):
            pl.when(has[way] == 1)(lambda way=way: halo_copy(way ^ 1, colour, half).wait_recv())

    def inlet_copy(j):
        return pltpu.make_async_remote_copy(
            src_ref=inlet.at[0],
            dst_ref=table.at[own],
            send_sem=slot_sem.at[j],
            recv_sem=interface_sem.at[0],
            device_id={"gx": n_gx - 1, "gy": j, "sa": 0},
            device_id_type=MESH,
        )

    def row_copy(g):
        return pltpu.make_async_remote_copy(
            src_ref=rows.at[g],
            dst_ref=arrived.at[gy],
            send_sem=slot_sem.at[g],
            recv_sem=interface_sem.at[1],
            device_id={"gx": g // n_gy, "gy": g % n_gy, "sa": 1},
            device_id_type=MESH,
        )

    @pl.when(has[0] == 0)
    def _():
        halo_x[0, 0] = jnp.zeros((states, cells_y, cells_z), jnp.float32)

    @pl.when((has[1] == 0) & turbine)
    def _():
        halo_x[1, 0] = jnp.zeros((states, cells_y, cells_z), jnp.float32)

    for side in range(2):
        @pl.when(has[2 + side] == 0)
        def _():
            halo_y[side, 0] = jnp.zeros((pairs, states, 1, cells_z), jnp.float32)

    load_fields.wait()
    for k in range(states):
        for p in range(pairs):
            held[0, p, k], held[1, p, k] = split(raw[k, 2 * p], raw[k, 2 * p + 1])
    stage_y(1)

    @pl.when(turbine)
    def _():
        row = jnp.zeros((cells_y, LANES), jnp.float32)
        for x in range(cells_x):
            row = jnp.where(lane % BLK == x * cells_y + sub, raw[0, x, :, 0:1], row)
        inlet[0] = jnp.sum(row, axis=0, keepdims=True)

    @pl.when(at_exit)
    def _():
        slot_row = lax.broadcasted_iota(jnp.int32, (slots, LANES), 0)
        in_state = tall * per_row + wide // BLK

        def take(e, total):
            block = jnp.where(donors[e, 0] == gy, donors[e, 1], -1)
            found = jnp.zeros((cells_y, cells_z), jnp.float32)
            for k in range(states):
                here = in_state == block - k * (cells_y * per_row)
                found = jnp.where(here, raw[k, cells_x - 1], found)
            row = jnp.sum(found, axis=0, keepdims=True)
            row = sum(row[:, i * LANES : (i + 1) * LANES] for i in range(cells_z // LANES))
            return jnp.where(slot_row == donors[e, 2], row, total)

        total = lax.fori_loop(0, slots, take, jnp.zeros((slots, LANES), jnp.float32))
        for g in range(slots):
            rows[g] = total[g : g + 1]

    met = has[0] + has[1] + has[2] + has[3] + sa * n_gy + (1 - sa) * (1 - has[1]) * slots
    pl.semaphore_wait(barrier, met)
    send(range(4), 1, 0)

    @pl.when(turbine)
    def _():
        for j in range(n_gy):
            inlet_copy(j).start()

    @pl.when(at_exit)
    def _():
        for g in range(slots):
            row_copy(g).start()

        spread_from = lax.broadcasted_iota(jnp.int32, (LANES, cells_z), 0) % per_row
        spread_to = lax.broadcasted_iota(jnp.int32, (LANES, cells_z), 1) // BLK
        spread = jnp.where(spread_from == spread_to, 1.0, 0.0)
        for k in range(states):
            ids = returns[0:1, k * LANES : (k + 1) * LANES].astype(jnp.float32)
            ids = jnp.where(lane // per_row == sub, ids, 0.0)
            wanted[k] = jnp.dot(
                ids, spread, precision=lax.Precision.HIGHEST, preferred_element_type=jnp.float32
            )

    load_source.wait()
    for k in range(states):
        for p in range(pairs):
            source[0, p, k], source[1, p, k] = split(raw_source[k, 2 * p], raw_source[k, 2 * p + 1])

    @pl.when(combustor)
    def _():
        load_diagonal.wait()
        for k in range(states):
            for p in range(pairs):
                first, second = split(raw_diagonal[k, 2 * p], raw_diagonal[k, 2 * p + 1])
                scale[0, p, k] = 1.0 / (6.0 + first)
                scale[1, p, k] = 1.0 / (6.0 + second)

    @pl.when(turbine)
    def _():
        load_inverse.wait()

        def pack(s, carry):
            for t in range(states):
                for p in range(pairs):
                    first, second = split(raw_inverse[s, t, 2 * p], raw_inverse[s, t, 2 * p + 1])
                    matrix[0, p, t, s] = first
                    matrix[1, p, t, s] = second
            return carry

        lax.fori_loop(0, states, pack, 0)

    def inner_terms(colour, section):
        other = 1 - colour
        upward = parity == 1 - colour
        for p in range(pairs):
            values = [held[other, p, k] for k in range(states)]
            lower = [pltpu.roll(value, 1, 1) for value in values]
            upper = [pltpu.roll(value, cells_z - 1, 1) for value in values]
            for k in range(states):
                if section == 0:
                    before = lower[k - 1] if k > 0 else 0.0
                    after = upper[k + 1] if k < states - 1 else 0.0
                else:
                    before = held[colour, p, k, :, 0:1] if k > 0 else 0.0
                    after = 0.0
                total = values[k]
                total += jnp.where(wide == 0, before, lower[k])
                total += jnp.where(wide == cells_z - 1, after, upper[k])
                total += jnp.where(tall == 0, 0.0, pltpu.roll(values[k], 1, 0))
                total += jnp.where(tall == cells_y - 1, 0.0, pltpu.roll(values[k], cells_y - 1, 0))
                next_pair = held[other, p + 1, k] if p < pairs - 1 else 0.0
                past_pair = held[other, p - 1, k] if p > 0 else 0.0
                total += jnp.where(upward, next_pair, past_pair)
                if section == 0:
                    total += source[colour, p, k]
                part[p, k] = total

    def halo_terms(colour, half, p, tile):
        lanes = pl.ds(tile * LANES, LANES)
        total = part[p, :, :, lanes]
        upward = jnp.logical_not(even_lanes) if colour == 0 else even_lanes
        if p == 0:
            total += jnp.where(upward, 0.0, halo_x[0, half * has[0], :, :, lanes])
        if p == pairs - 1:
            total += jnp.where(upward, halo_x[1, half * has[1], :, :, lanes], 0.0)
        total += jnp.where(sub == 0, halo_y[0, half * has[2], p, :, :, lanes], 0.0)
        total += jnp.where(sub == cells_y - 1, halo_y[1, half * has[3], p, :, :, lanes], 0.0)
        return total

    def half_sweep(colour, half, section):
        other = 1 - colour
        inner_terms(colour, section)
        wait_received(other, half)
        if colour == 0 and section == 0:
            @pl.when((half == 0) & at_exit)
            def _():
                pltpu.make_async_copy(table, table, interface_sem.at[0]).wait()

                def lay(k, carry):
                    ids = wanted[k]
                    plane = jnp.zeros((cells_y, cells_z), jnp.float32)
                    for g in range(slots):
                        row = jnp.concatenate([table[g]] * (cells_z // LANES), axis=1)
                        plane = jnp.where(ids == float(g), row, plane)
                    halo_x[1, 0, k] = plane
                    return carry

                lax.fori_loop(0, states, lay, 0)

        if colour == 0 and section == 1:
            @pl.when(half == 0)
            def _():
                pltpu.make_async_copy(arrived, arrived, interface_sem.at[1]).wait()
                row = arrived[0]
                for j in range(1, n_gy):
                    row = row + arrived[j]
                columns = [
                    jnp.sum(
                        jnp.where(lane % BLK == x * cells_y + sub, row, 0.0), axis=1, keepdims=True
                    )
                    for x in range(cells_x)
                ]
                for p in range(pairs):
                    for c in range(2):
                        cell = jnp.where(sub % 2 == c, columns[2 * p], columns[2 * p + 1])
                        inflow[c, p] = jnp.where(lane == 0, cell, 0.0)

        for p in range(pairs):
            for tile in range(cells_z // LANES):
                lanes = pl.ds(tile * LANES, LANES)
                total = halo_terms(colour, half, p, tile)
                if section == 0:
                    held[colour, p, :, :, lanes] = total * scale[colour, p, :, :, lanes]
                    continue
                result = None
                for t in range(states):
                    summed = total[t]
                    if t == 0 and tile == 0:
                        summed = summed + inflow[colour, p]
                    driving = source[colour, p, t, :, lanes] + coupling[t] * summed
                    term = matrix[colour, p, t, :, :, lanes] * driving
                    result = term if result is None else result + term
                held[colour, p, :, :, lanes] = result
            if p == 0:
                pl.when(half < halves - 1)(lambda: send((0,), colour, half + 1))

        @pl.when(half < halves - 1)
        def _():
            send((1,), colour, half + 1)
            stage_y(colour)
            send((2, 3), colour, half + 1)

        wait_sent(other, half)

    for section in range(2):
        @pl.when(sa == section)
        def _():
            def sweep(index, carry):
                half_sweep(0, 2 * index, section)
                half_sweep(1, 2 * index + 1, section)
                return carry

            lax.fori_loop(0, SWEEPS, sweep, 0)

    for k in range(states):
        for p in range(pairs):
            first, second = split(held[0, p, k], held[1, p, k])
            out[0, k, 2 * p] = first
            out[0, k, 2 * p + 1] = second

    @pl.when(turbine)
    def _():
        for j in range(n_gy):
            inlet_copy(j).wait_send()

    @pl.when(at_exit)
    def _():
        for g in range(slots):
            row_copy(g).wait_send()


def shards(n_gx, n_gy, fields, sources, diagonal, block_inverse, coupling, donors, returns):
    _, states, cells_x, cells_y, cells_z = fields.shape
    pairs = cells_x // 2
    slots = donors.shape[0]
    assert cells_x % 2 == 0 and cells_y % 2 == 0 and cells_x * cells_y == BLK
    assert cells_y * cells_z == LANES * BLK and slots == n_gx * n_gy
    f32 = jnp.float32
    block = (states, cells_x, cells_y, cells_z)
    halves = 2 * SWEEPS
    anywhere = pl.BlockSpec(memory_space=pl.ANY)
    vmem = pl.BlockSpec(memory_space=pltpu.VMEM)
    smem = pl.BlockSpec(memory_space=pltpu.SMEM)
    by_colour = (2, pairs, states, cells_y, cells_z)
    return pl.pallas_call(
        functools.partial(kernel, n_gx, n_gy, block),
        out_shape=jax.ShapeDtypeStruct(fields.shape, f32),
        in_specs=[anywhere, anywhere, anywhere, anywhere, smem, smem, vmem],
        out_specs=vmem,
        scratch_shapes=[
            pltpu.VMEM(block, f32),
            pltpu.VMEM(block, f32),
            pltpu.VMEM(block, f32),
            pltpu.VMEM((states,) + block, f32),
            pltpu.VMEM(by_colour, f32),
            pltpu.VMEM(by_colour, f32),
            pltpu.VMEM(by_colour, f32),
            pltpu.VMEM((2, pairs, states, states, cells_y, cells_z), f32),
            pltpu.VMEM(by_colour[1:], f32),
            pltpu.VMEM((2, halves, states, cells_y, cells_z), f32),
            pltpu.VMEM((2, halves, pairs, states, 1, cells_z), f32),
            pltpu.VMEM((2, 2, pairs, states, 1, cells_z), f32),
            pltpu.VMEM((2, pairs, cells_y, LANES), f32),
            pltpu.VMEM((states, cells_y, cells_z), f32),
            pltpu.VMEM((slots, 1, LANES), f32),
            pltpu.VMEM((slots, 1, LANES), f32),
            pltpu.VMEM((1, 1, LANES), f32),
            pltpu.VMEM((n_gy, 1, LANES), f32),
            pltpu.SemaphoreType.DMA((4,)),
            pltpu.SemaphoreType.DMA((4, halves)),
            pltpu.SemaphoreType.DMA((4, halves)),
            pltpu.SemaphoreType.DMA((slots,)),
            pltpu.SemaphoreType.DMA((2,)),
        ],
        compiler_params=pltpu.CompilerParams(
            collective_id=0, has_side_effects=True, vmem_limit_bytes=32 * 1024 * 1024
        ),
    )(fields, sources, diagonal, block_inverse, coupling, donors, returns)


def solution(mesh):
    return jax.shard_map(
        functools.partial(shards, mesh.shape["gx"], mesh.shape["gy"]),
        mesh=mesh,
        in_specs=(
            P("sa", None, "gx", "gy", None),
            P("sa", None, "gx", "gy", None),
            P(None, "gx", "gy", None),
            P(None, None, "gx", "gy", None),
            P(),
            P(),
            P("gy", None),
        ),
        out_specs=P("sa", None, "gx", "gy", None),
        check_vma=False,
    )
```

```python
import functools

import jax
import jax.numpy as jnp
from jax import lax
from jax.experimental import pallas as pl
from jax.experimental.pallas import tpu as pltpu
from jax.sharding import PartitionSpec as P

SWEEPS = 4
BLK = 32
LANES = 128
MESH = pl.DeviceIdType.MESH
CHUNKS = 2


def kernel(
    n_gx, n_gy, sizes,
    fields, sources, diagonal, inverse, coupling, donors, returns, out,
    raw, raw_source, raw_diagonal, raw_inverse, weights, list_of, returned,
    held, source, scale, matrix, part,
    halo_x, halo_y, edge_x, edge_y, inflow, wanted, table, rows, inlet, arrived,
    local_sem, send_sem, recv_sem, slot_sem, interface_sem,
):
    states, cells_x, cells_y, cells_z = sizes
    pairs = cells_x // 2
    halves = 2 * SWEEPS
    slots = n_gx * n_gy
    per_row = cells_z // BLK
    packs = (states + 1) // 2
    tiles = cells_z // LANES
    chunk_tiles = tiles // CHUNKS
    gx, gy, sa = lax.axis_index("gx"), lax.axis_index("gy"), lax.axis_index("sa")
    own = gx * n_gy + gy
    has = (
        (gx + n_gx - 1) // n_gx,
        1 - (gx + 1) // n_gx,
        (gy + n_gy - 1) // n_gy,
        1 - (gy + 1) // n_gy,
    )
    peers = ({"gx": gx - 1}, {"gx": gx + 1}, {"gy": gy - 1}, {"gy": gy + 1})
    combustor = sa == 0
    turbine = sa == 1
    at_exit = combustor & (gx == n_gx - 1)

    load_fields = pltpu.make_async_copy(fields.at[0], raw, local_sem.at[0])
    load_source = pltpu.make_async_copy(sources.at[0], raw_source, local_sem.at[1])
    load_diagonal = pltpu.make_async_copy(diagonal, raw_diagonal, local_sem.at[2])
    load_inverse = pltpu.make_async_copy(inverse, raw_inverse, local_sem.at[3])
    load_lists = pltpu.make_async_copy(donors, list_of, local_sem.at[4])
    load_returns = pltpu.make_async_copy(returns, returned, local_sem.at[5])
    load_weights = pltpu.make_async_copy(coupling, weights, local_sem.at[6])
    load_fields.start()
    pl.when(at_exit)(load_lists.start)
    pl.when(at_exit)(load_returns.start)
    load_source.start()
    pl.when(turbine)(load_weights.start)
    pl.when(combustor)(load_diagonal.start)
    pl.when(turbine)(load_inverse.start)

    barrier = pltpu.get_barrier_semaphore()

    def greet(peer):
        pl.semaphore_signal(barrier, inc=1, device_id=peer, device_id_type=MESH)

    for there, peer in zip(has, peers):
        pl.when(there == 1)(functools.partial(greet, peer))

    @pl.when(turbine)
    def _():
        for j in range(n_gy):
            greet({"gx": n_gx - 1, "gy": j, "sa": 0})

    @pl.when(at_exit)
    def _():
        for g in range(slots):
            greet({"gx": g // n_gy, "gy": g % n_gy, "sa": 1})

    sub = lax.broadcasted_iota(jnp.int32, (cells_y, LANES), 0)
    lane = lax.broadcasted_iota(jnp.int32, (cells_y, LANES), 1)
    tall = lax.broadcasted_iota(jnp.int32, (cells_y, cells_z), 0)
    wide = lax.broadcasted_iota(jnp.int32, (cells_y, cells_z), 1)
    parity = (tall + wide) % 2
    even = parity == 0
    even_lanes = (sub + lane) % 2 == 0

    def split(even_plane, odd_plane):
        return (jnp.where(even, even_plane, odd_plane), jnp.where(even, odd_plane, even_plane))

    def pack_x(values, chosen):
        moved = [pltpu.roll(values[k], 1, 0) for k in range(packs, states)]
        moved += [values[k] for k in range(states - packs, packs)]
        return [jnp.where(chosen, values[k], moved[k]) for k in range(packs)]

    def stage(colour, p, tile, values):
        at = (tile // chunk_tiles, tile % chunk_tiles)
        faces = [(0, even_lanes == (colour == 0))] if p == 0 else []
        faces += [(1, even_lanes == (colour == 1))] if p == pairs - 1 else []
        for way, chosen in faces:
            for k, packed in enumerate(pack_x(values, chosen)):
                edge_x[way, colour, at[0], at[1], k] = packed
        for k in range(states):
            edge_y[0, colour, at[0], at[1], p, k] = values[k][0:1]
            edge_y[1, colour, at[0], at[1], p, k] = values[k][cells_y - 1 : cells_y]

    def halo_copy(way, colour, half, chunk):
        edges, halos = (edge_x, halo_x) if way < 2 else (edge_y, halo_y)
        return pltpu.make_async_remote_copy(
            src_ref=edges.at[way % 2, colour, chunk],
            dst_ref=halos.at[1 - way % 2, half, chunk],
            send_sem=send_sem.at[way, half, chunk],
            recv_sem=recv_sem.at[way, half, chunk],
            device_id=peers[way],
            device_id_type=MESH,
        )

    def send(colour, half, chunk):
        for way in range(4):
            pl.when(has[way] == 1)(lambda way=way: halo_copy(way, colour, half, chunk).start())

    def wait_sent(colour, half):
        for way in range(4):
            @pl.when(has[way] == 1)
            def _():
                for chunk in range(CHUNKS):
                    halo_copy(way, colour, half, chunk).wait_send()

    def wait_received(colour, half, chunk):
        for way in range(4):
            pl.when(has[way] == 1)(
                lambda way=way: halo_copy(way ^ 1, colour, half, chunk).wait_recv()
            )

    def inlet_copy(j):
        return pltpu.make_async_remote_copy(
            src_ref=inlet.at[0],
            dst_ref=table.at[own],
            send_sem=slot_sem.at[j],
            recv_sem=interface_sem.at[0],
            device_id={"gx": n_gx - 1, "gy": j, "sa": 0},
            device_id_type=MESH,
        )

    def row_copy(g):
        return pltpu.make_async_remote_copy(
            src_ref=rows.at[g],
            dst_ref=arrived.at[gy],
            send_sem=slot_sem.at[g],
            recv_sem=interface_sem.at[1],
            device_id={"gx": g // n_gy, "gy": g % n_gy, "sa": 1},
            device_id_type=MESH,
        )

    @pl.when(has[0] == 0)
    def _():
        halo_x[0, 0:2] = jnp.zeros((2,) + halo_x.shape[2:], jnp.float32)

    @pl.when((has[1] == 0) & turbine)
    def _():
        halo_x[1, 0:2] = jnp.zeros((2,) + halo_x.shape[2:], jnp.float32)

    for side in range(2):
        @pl.when(has[2 + side] == 0)
        def _():
            halo_y[side, 0:2] = jnp.zeros((2,) + halo_y.shape[2:], jnp.float32)

    load_fields.wait()
    for k in range(states):
        for p in range(pairs):
            held[0, p, k], held[1, p, k] = split(raw[k, 2 * p], raw[k, 2 * p + 1])
    for tile in range(tiles):
        lanes = pl.ds(tile * LANES, LANES)
        for p in range(pairs):
            stage(1, p, tile, [held[1, p, k, :, lanes] for k in range(states)])

    @pl.when(turbine)
    def _():
        row = jnp.zeros((cells_y, LANES), jnp.float32)
        for x in range(cells_x):
            row = jnp.where(lane % BLK == x * cells_y + sub, raw[0, x, :, 0:1], row)
        inlet[0] = jnp.sum(row, axis=0, keepdims=True)

    @pl.when(at_exit)
    def _():
        load_lists.wait()
        slot_row = lax.broadcasted_iota(jnp.int32, (slots, LANES), 0)
        in_state = tall * per_row + wide // BLK

        def take(e, total):
            block = jnp.where(list_of[0, e] == gy, list_of[1, e], -1)
            found = jnp.zeros((cells_y, cells_z), jnp.float32)
            for k in range(states):
                here = in_state == block - k * (cells_y * per_row)
                found = jnp.where(here, raw[k, cells_x - 1], found)
            row = jnp.sum(found, axis=0, keepdims=True)
            row = sum(row[:, i * LANES : (i + 1) * LANES] for i in range(cells_z // LANES))
            return jnp.where(slot_row == list_of[2, e], row, total)

        total = lax.fori_loop(0, slots, take, jnp.zeros((slots, LANES), jnp.float32))
        for g in range(slots):
            rows[g] = total[g : g + 1]

    met = has[0] + has[1] + has[2] + has[3] + sa * n_gy + (1 - sa) * (1 - has[1]) * slots
    pl.semaphore_wait(barrier, met)
    for chunk in range(CHUNKS):
        send(1, 0, chunk)

    @pl.when(turbine)
    def _():
        for j in range(n_gy):
            inlet_copy(j).start()

    @pl.when(at_exit)
    def _():
        for g in range(slots):
            row_copy(g).start()

        spread_from = lax.broadcasted_iota(jnp.int32, (LANES, cells_z), 0) % per_row
        spread_to = lax.broadcasted_iota(jnp.int32, (LANES, cells_z), 1) // BLK
        spread = jnp.where(spread_from == spread_to, 1.0, 0.0)
        load_returns.wait()
        for k in range(states):
            ids = returned[0:1, k * LANES : (k + 1) * LANES].astype(jnp.float32)
            ids = jnp.where(lane // per_row == sub, ids, 0.0)
            wanted[k] = jnp.dot(
                ids, spread, precision=lax.Precision.HIGHEST, preferred_element_type=jnp.float32
            )

    load_source.wait()
    for k in range(states):
        for p in range(pairs):
            source[0, p, k], source[1, p, k] = split(raw_source[k, 2 * p], raw_source[k, 2 * p + 1])

    @pl.when(combustor)
    def _():
        load_diagonal.wait()
        for k in range(states):
            for p in range(pairs):
                first, second = split(raw_diagonal[k, 2 * p], raw_diagonal[k, 2 * p + 1])
                scale[0, p, k] = 1.0 / (6.0 + first)
                scale[1, p, k] = 1.0 / (6.0 + second)

    @pl.when(turbine)
    def _():
        load_weights.wait()
        load_inverse.wait()

        def pack(s, carry):
            for t in range(states):
                for p in range(pairs):
                    first, second = split(raw_inverse[s, t, 2 * p], raw_inverse[s, t, 2 * p + 1])
                    matrix[0, p, t, s] = first
                    matrix[1, p, t, s] = second
            return carry

        lax.fori_loop(0, states, pack, 0)

    def inner_terms(colour, section):
        other = 1 - colour
        upward = parity == 1 - colour
        for p in range(pairs):
            values = [held[other, p, k] for k in range(states)]
            lower = [pltpu.roll(value, 1, 1) for value in values]
            upper = [pltpu.roll(value, cells_z - 1, 1) for value in values]
            for k in range(states):
                if section == 0:
                    before = lower[k - 1] if k > 0 else 0.0
                    after = upper[k + 1] if k < states - 1 else 0.0
                else:
                    before = held[colour, p, k, :, 0:1] if k > 0 else 0.0
                    after = 0.0
                total = values[k]
                total += jnp.where(wide == 0, before, lower[k])
                total += jnp.where(wide == cells_z - 1, after, upper[k])
                total += jnp.where(tall == 0, 0.0, pltpu.roll(values[k], 1, 0))
                total += jnp.where(tall == cells_y - 1, 0.0, pltpu.roll(values[k], cells_y - 1, 0))
                next_pair = held[other, p + 1, k] if p < pairs - 1 else 0.0
                past_pair = held[other, p - 1, k] if p > 0 else 0.0
                total += jnp.where(upward, next_pair, past_pair)
                if section == 0:
                    total += source[colour, p, k]
                part[p, k] = total

    def halo_terms(colour, half, p, tile):
        lanes = pl.ds(tile * LANES, LANES)
        at = (tile // chunk_tiles, tile % chunk_tiles)
        totals = [part[p, k, :, lanes] for k in range(states)]
        upward = even_lanes == (colour == 1)
        slot = [half * there + colour * (1 - there) for there in has]
        for side in ([0] if p == 0 else []) + ([1] if p == pairs - 1 else []):
            for k in range(packs):
                packed = halo_x[side, slot[side], at[0], at[1], k]
                chosen = upward if side == 1 else jnp.logical_not(upward)
                totals[k] += jnp.where(chosen, packed, 0.0)
                if k + packs < states:
                    back = pltpu.roll(packed, cells_y - 1, 0)
                    totals[k + packs] += jnp.where(chosen, back, 0.0)
        for k in range(states):
            below = halo_y[0, slot[2], at[0], at[1], p, k]
            above = halo_y[1, slot[3], at[0], at[1], p, k]
            totals[k] += jnp.where(sub == 0, below, jnp.where(sub == cells_y - 1, above, 0.0))
        return totals

    def half_sweep(colour, half, section):
        other = 1 - colour
        inner_terms(colour, section)
        wait_received(other, half, 0)
        if colour == 0 and section == 0:
            @pl.when((half == 0) & at_exit)
            def _():
                pltpu.make_async_copy(table, table, interface_sem.at[0]).wait()

                def lay(k, carry):
                    ids = wanted[k]
                    plane = jnp.zeros((cells_y, cells_z), jnp.float32)
                    for g in range(slots):
                        row = jnp.concatenate([table[g]] * (cells_z // LANES), axis=1)
                        plane = jnp.where(ids == float(g), row, plane)
                    wanted[k] = plane
                    return carry

                lax.fori_loop(0, states, lay, 0)
                for tile in range(tiles):
                    lanes = pl.ds(tile * LANES, LANES)
                    planes = [wanted[k, :, lanes] for k in range(states)]
                    for c in range(2):
                        for k, packed in enumerate(pack_x(planes, even_lanes == (c == 1))):
                            halo_x[1, c, tile // chunk_tiles, tile % chunk_tiles, k] = packed

        if colour == 0 and section == 1:
            @pl.when(half == 0)
            def _():
                pltpu.make_async_copy(arrived, arrived, interface_sem.at[1]).wait()
                row = arrived[0]
                for j in range(1, n_gy):
                    row = row + arrived[j]
                columns = [
                    jnp.sum(
                        jnp.where(lane % BLK == x * cells_y + sub, row, 0.0), axis=1, keepdims=True
                    )
                    for x in range(cells_x)
                ]
                for p in range(pairs):
                    for c in range(2):
                        cell = jnp.where(sub % 2 == c, columns[2 * p], columns[2 * p + 1])
                        inflow[c, p] = jnp.where(lane == 0, cell, 0.0)

        for chunk in range(CHUNKS):
            if chunk > 0:
                wait_received(other, half, chunk)
            for tile in range(chunk * chunk_tiles, (chunk + 1) * chunk_tiles):
                lanes = pl.ds(tile * LANES, LANES)
                for p in range(pairs):
                    totals = halo_terms(colour, half, p, tile)
                    if section == 0:
                        results = [totals[k] * scale[colour, p, k, :, lanes] for k in range(states)]
                    else:
                        if tile == 0:
                            totals[0] += inflow[colour, p]
                        result = None
                        for t in range(states):
                            driving = source[colour, p, t, :, lanes] + weights[t] * totals[t]
                            term = matrix[colour, p, t, :, :, lanes] * driving
                            result = term if result is None else result + term
                        results = [result[k] for k in range(states)]
                    for k in range(states):
                        held[colour, p, k, :, lanes] = results[k]
                    stage(colour, p, tile, results)
            pl.when(half < halves - 1)(functools.partial(send, colour, half + 1, chunk))

        wait_sent(other, half)

    for section in range(2):
        @pl.when(sa == section)
        def _():
            def sweep(index, carry):
                half_sweep(0, 2 * index, section)
                half_sweep(1, 2 * index + 1, section)
                return carry

            lax.fori_loop(0, SWEEPS, sweep, 0)

    for k in range(states):
        for p in range(pairs):
            first, second = split(held[0, p, k], held[1, p, k])
            out[0, k, 2 * p] = first
            out[0, k, 2 * p + 1] = second

    @pl.when(turbine)
    def _():
        for j in range(n_gy):
            inlet_copy(j).wait_send()

    @pl.when(at_exit)
    def _():
        for g in range(slots):
            row_copy(g).wait_send()


def shards(n_gx, n_gy, fields, sources, diagonal, block_inverse, coupling, donors, returns):
    _, states, cells_x, cells_y, cells_z = fields.shape
    pairs = cells_x // 2
    slots = donors.shape[0]
    assert cells_x % 2 == 0 and cells_y % 2 == 0 and cells_x * cells_y == BLK
    assert cells_y * cells_z == LANES * BLK and slots == n_gx * n_gy
    f32 = jnp.float32
    block = (states, cells_x, cells_y, cells_z)
    halves = 2 * SWEEPS
    tiles = cells_z // LANES
    packs = (states + 1) // 2
    chunk = (CHUNKS, tiles // CHUNKS)
    hbm = pl.BlockSpec(memory_space=pltpu.HBM)
    vmem = pl.BlockSpec(memory_space=pltpu.VMEM)
    by_colour = (2, pairs, states, cells_y, cells_z)
    return pl.pallas_call(
        functools.partial(kernel, n_gx, n_gy, block),
        out_shape=jax.ShapeDtypeStruct(fields.shape, f32),
        in_specs=[hbm] * 7,
        out_specs=vmem,
        scratch_shapes=[
            pltpu.VMEM(block, f32),
            pltpu.VMEM(block, f32),
            pltpu.VMEM(block, f32),
            pltpu.VMEM((states,) + block, f32),
            pltpu.SMEM(coupling.shape, f32),
            pltpu.SMEM(donors.shape[::-1], jnp.int32),
            pltpu.VMEM(returns.shape, jnp.int32),
            pltpu.VMEM(by_colour, f32),
            pltpu.VMEM(by_colour, f32),
            pltpu.VMEM(by_colour, f32),
            pltpu.VMEM((2, pairs, states, states, cells_y, cells_z), f32),
            pltpu.VMEM(by_colour[1:], f32),
            pltpu.VMEM((2, halves) + chunk + (packs, cells_y, LANES), f32),
            pltpu.VMEM((2, halves) + chunk + (pairs, states, 1, LANES), f32),
            pltpu.VMEM((2, 2) + chunk + (packs, cells_y, LANES), f32),
            pltpu.VMEM((2, 2) + chunk + (pairs, states, 1, LANES), f32),
            pltpu.VMEM((2, pairs, cells_y, LANES), f32),
            pltpu.VMEM((states, cells_y, cells_z), f32),
            pltpu.VMEM((slots, 1, LANES), f32),
            pltpu.VMEM((slots, 1, LANES), f32),
            pltpu.VMEM((1, 1, LANES), f32),
            pltpu.VMEM((n_gy, 1, LANES), f32),
            pltpu.SemaphoreType.DMA((7,)),
            pltpu.SemaphoreType.DMA((4, halves, CHUNKS)),
            pltpu.SemaphoreType.DMA((4, halves, CHUNKS)),
            pltpu.SemaphoreType.DMA((slots,)),
            pltpu.SemaphoreType.DMA((2,)),
        ],
        compiler_params=pltpu.CompilerParams(
            collective_id=0, has_side_effects=True, vmem_limit_bytes=60 * 1024 * 1024
        ),
    )(fields, sources, diagonal, block_inverse, coupling, donors.T, returns)


def solution(mesh):
    return jax.shard_map(
        functools.partial(shards, mesh.shape["gx"], mesh.shape["gy"]),
        mesh=mesh,
        in_specs=(
            P("sa", None, "gx", "gy", None),
            P("sa", None, "gx", "gy", None),
            P(None, "gx", "gy", None),
            P(None, None, "gx", "gy", None),
            P(),
            P(),
            P("gy", None),
        ),
        out_specs=P("sa", None, "gx", "gy", None),
        check_vma=False,
    )
```

```python
import functools

import jax
import jax.numpy as jnp
from jax import lax
from jax.experimental import pallas as pl
from jax.experimental.pallas import tpu as pltpu
from jax.sharding import PartitionSpec as P

SWEEPS = 4
BLK = 32
LANES = 128
MESH = pl.DeviceIdType.MESH
CHUNKS = 2
X_WAYS, Y_WAYS = (0, 1), (2, 3)
PLANES = ((0, 3), (2, 1))


def kernel(
    n_gx, n_gy, sizes,
    fields, sources, diagonal, inverse, coupling, donors, returns, out,
    raw, raw_source, raw_diagonal, raw_inverse, weights, list_of, returned,
    held, source, scale, matrix, part,
    halo_x, halo_y, edge_x, edge_y, inflow, wanted, table, rows, inlet, arrived,
    local_sem, send_sem, recv_sem, slot_sem, interface_sem,
):
    states, cells_x, cells_y, cells_z = sizes
    pairs = len(PLANES)
    halves = 2 * SWEEPS
    slots = n_gx * n_gy
    per_row = cells_z // BLK
    packs = (states + 1) // 2
    tiles = cells_z // LANES
    chunk_tiles = tiles // CHUNKS
    gx, gy, sa = lax.axis_index("gx"), lax.axis_index("gy"), lax.axis_index("sa")
    own = gx * n_gy + gy
    has = (
        (gx + n_gx - 1) // n_gx,
        1 - (gx + 1) // n_gx,
        (gy + n_gy - 1) // n_gy,
        1 - (gy + 1) // n_gy,
    )
    peers = ({"gx": gx - 1}, {"gx": gx + 1}, {"gy": gy - 1}, {"gy": gy + 1})
    combustor = sa == 0
    turbine = sa == 1
    at_exit = combustor & (gx == n_gx - 1)

    load_fields = pltpu.make_async_copy(fields.at[0], raw, local_sem.at[0])
    load_source = pltpu.make_async_copy(sources.at[0], raw_source, local_sem.at[1])
    load_diagonal = pltpu.make_async_copy(diagonal, raw_diagonal, local_sem.at[2])
    load_inverse = pltpu.make_async_copy(inverse, raw_inverse, local_sem.at[3])
    load_lists = pltpu.make_async_copy(donors, list_of, local_sem.at[4])
    load_returns = pltpu.make_async_copy(returns, returned, local_sem.at[5])
    load_weights = pltpu.make_async_copy(coupling, weights, local_sem.at[6])
    load_fields.start()
    pl.when(at_exit)(load_lists.start)
    pl.when(at_exit)(load_returns.start)
    load_source.start()
    pl.when(turbine)(load_weights.start)
    pl.when(combustor)(load_diagonal.start)
    pl.when(turbine)(load_inverse.start)

    barrier = pltpu.get_barrier_semaphore()

    def greet(peer):
        pl.semaphore_signal(barrier, inc=1, device_id=peer, device_id_type=MESH)

    for there, peer in zip(has, peers):
        pl.when(there == 1)(functools.partial(greet, peer))

    @pl.when(turbine)
    def _():
        for j in range(n_gy):
            greet({"gx": n_gx - 1, "gy": j, "sa": 0})

    @pl.when(at_exit)
    def _():
        for g in range(slots):
            greet({"gx": g // n_gy, "gy": g % n_gy, "sa": 1})

    sub = lax.broadcasted_iota(jnp.int32, (cells_y, LANES), 0)
    lane = lax.broadcasted_iota(jnp.int32, (cells_y, LANES), 1)
    tall = lax.broadcasted_iota(jnp.int32, (cells_y, cells_z), 0)
    wide = lax.broadcasted_iota(jnp.int32, (cells_y, cells_z), 1)
    parity = (tall + wide) % 2
    even = parity == 0
    even_lanes = (sub + lane) % 2 == 0

    def split(even_plane, odd_plane):
        return (jnp.where(even, even_plane, odd_plane), jnp.where(even, odd_plane, even_plane))

    def split_planes(block, k, p):
        return split(block[k, PLANES[p][0]], block[k, PLANES[p][1]])

    def pack_x(values, *choices):
        moved = [pltpu.roll(values[k], 1, 0) for k in range(packs, states)]
        moved += [values[k] for k in range(states - packs, packs)]
        return [
            [jnp.where(chosen, values[k], moved[k]) for k in range(packs)] for chosen in choices
        ]

    def stage(colour, p, tile, values):
        if p == 0:
            faces = pack_x(values, even_lanes == (colour == 0), even_lanes == (colour == 1))
            for way in range(2):
                for k in range(packs):
                    at = (tile // chunk_tiles, tile % chunk_tiles)
                    edge_x[way, colour, at[0], at[1], k] = faces[way][k]
        for k in range(states):
            edge_y[0, colour, p, tile, k] = values[k][0:1]
            edge_y[1, colour, p, tile, k] = values[k][cells_y - 1 : cells_y]

    def halo_copy(way, colour, half, piece):
        edges, halos = (edge_x, halo_x) if way < 2 else (edge_y, halo_y)
        return pltpu.make_async_remote_copy(
            src_ref=edges.at[way % 2, colour, piece],
            dst_ref=halos.at[1 - way % 2, half, piece],
            send_sem=send_sem.at[way, half, piece],
            recv_sem=recv_sem.at[way, half, piece],
            device_id=peers[way],
            device_id_type=MESH,
        )

    def send(ways, colour, half, piece):
        for way in ways:
            pl.when(has[way] == 1)(lambda way=way: halo_copy(way, colour, half, piece).start())

    def wait_sent(colour, half):
        for way in range(4):
            @pl.when(has[way] == 1)
            def _():
                for piece in range(CHUNKS if way < 2 else pairs):
                    halo_copy(way, colour, half, piece).wait_send()

    def wait_received(ways, colour, half, piece):
        for way in ways:
            pl.when(has[way] == 1)(
                lambda way=way: halo_copy(way ^ 1, colour, half, piece).wait_recv()
            )

    def inlet_copy(j):
        return pltpu.make_async_remote_copy(
            src_ref=inlet.at[0],
            dst_ref=table.at[own],
            send_sem=slot_sem.at[j],
            recv_sem=interface_sem.at[0],
            device_id={"gx": n_gx - 1, "gy": j, "sa": 0},
            device_id_type=MESH,
        )

    def row_copy(g):
        return pltpu.make_async_remote_copy(
            src_ref=rows.at[g],
            dst_ref=arrived.at[gy],
            send_sem=slot_sem.at[g],
            recv_sem=interface_sem.at[1],
            device_id={"gx": g // n_gy, "gy": g % n_gy, "sa": 1},
            device_id_type=MESH,
        )

    @pl.when(has[0] == 0)
    def _():
        halo_x[0, 0:2] = jnp.zeros((2,) + halo_x.shape[2:], jnp.float32)

    @pl.when((has[1] == 0) & turbine)
    def _():
        halo_x[1, 0:2] = jnp.zeros((2,) + halo_x.shape[2:], jnp.float32)

    for side in range(2):
        @pl.when(has[2 + side] == 0)
        def _():
            halo_y[side, 0:2] = jnp.zeros((2,) + halo_y.shape[2:], jnp.float32)

    load_fields.wait()
    for k in range(states):
        for p in range(pairs):
            held[0, p, k], held[1, p, k] = split_planes(raw, k, p)
    for tile in range(tiles):
        lanes = pl.ds(tile * LANES, LANES)
        for p in range(pairs):
            stage(1, p, tile, [held[1, p, k, :, lanes] for k in range(states)])

    @pl.when(turbine)
    def _():
        row = jnp.zeros((cells_y, LANES), jnp.float32)
        for x in range(cells_x):
            row = jnp.where(lane % BLK == x * cells_y + sub, raw[0, x, :, 0:1], row)
        inlet[0] = jnp.sum(row, axis=0, keepdims=True)

    @pl.when(at_exit)
    def _():
        load_lists.wait()
        slot_row = lax.broadcasted_iota(jnp.int32, (slots, LANES), 0)
        in_state = tall * per_row + wide // BLK

        def take(e, total):
            block = jnp.where(list_of[0, e] == gy, list_of[1, e], -1)
            found = jnp.zeros((cells_y, cells_z), jnp.float32)
            for k in range(states):
                here = in_state == block - k * (cells_y * per_row)
                found = jnp.where(here, raw[k, cells_x - 1], found)
            row = jnp.sum(found, axis=0, keepdims=True)
            row = sum(row[:, i * LANES : (i + 1) * LANES] for i in range(cells_z // LANES))
            return jnp.where(slot_row == list_of[2, e], row, total)

        total = lax.fori_loop(0, slots, take, jnp.zeros((slots, LANES), jnp.float32))
        for g in range(slots):
            rows[g] = total[g : g + 1]

    met = has[0] + has[1] + has[2] + has[3] + sa * n_gy + (1 - sa) * (1 - has[1]) * slots
    pl.semaphore_wait(barrier, met)
    for chunk in range(CHUNKS):
        send(X_WAYS, 1, 0, chunk)
    for p in range(pairs):
        send(Y_WAYS, 1, 0, p)

    @pl.when(turbine)
    def _():
        for j in range(n_gy):
            inlet_copy(j).start()

    @pl.when(at_exit)
    def _():
        for g in range(slots):
            row_copy(g).start()

        spread_from = lax.broadcasted_iota(jnp.int32, (LANES, cells_z), 0) % per_row
        spread_to = lax.broadcasted_iota(jnp.int32, (LANES, cells_z), 1) // BLK
        spread = jnp.where(spread_from == spread_to, 1.0, 0.0)
        load_returns.wait()
        for k in range(states):
            ids = returned[0:1, k * LANES : (k + 1) * LANES].astype(jnp.float32)
            ids = jnp.where(lane // per_row == sub, ids, 0.0)
            wanted[k] = jnp.dot(
                ids, spread, precision=lax.Precision.HIGHEST, preferred_element_type=jnp.float32
            )

    load_source.wait()
    for k in range(states):
        for p in range(pairs):
            source[0, p, k], source[1, p, k] = split_planes(raw_source, k, p)

    @pl.when(combustor)
    def _():
        load_diagonal.wait()
        for k in range(states):
            for p in range(pairs):
                first, second = split_planes(raw_diagonal, k, p)
                scale[0, p, k] = 1.0 / (6.0 + first)
                scale[1, p, k] = 1.0 / (6.0 + second)

    @pl.when(turbine)
    def _():
        load_weights.wait()
        load_inverse.wait()

        def pack(s, carry):
            for t in range(states):
                for p in range(pairs):
                    first, second = split_planes(raw_inverse.at[s], t, p)
                    matrix[0, p, t, s] = first
                    matrix[1, p, t, s] = second
            return carry

        lax.fori_loop(0, states, pack, 0)

    def inner_terms(colour, section):
        other = 1 - colour
        for p in range(pairs):
            values = [held[other, p, k] for k in range(states)]
            lower = [pltpu.roll(value, 1, 1) for value in values]
            upper = [pltpu.roll(value, cells_z - 1, 1) for value in values]
            for k in range(states):
                if section == 0:
                    before = lower[k - 1] if k > 0 else 0.0
                    after = upper[k + 1] if k < states - 1 else 0.0
                else:
                    before = held[colour, p, k, :, 0:1] if k > 0 else 0.0
                    after = 0.0
                total = held[other, 1, k]
                if p == 1:
                    total += held[other, 0, k]
                total += jnp.where(wide == 0, before, lower[k])
                total += jnp.where(wide == cells_z - 1, after, upper[k])
                total += jnp.where(tall == 0, 0.0, pltpu.roll(values[k], 1, 0))
                total += jnp.where(tall == cells_y - 1, 0.0, pltpu.roll(values[k], cells_y - 1, 0))
                if section == 0:
                    total += source[colour, p, k]
                part[p, k] = total

    def halo_terms(colour, half, p, tile):
        lanes = pl.ds(tile * LANES, LANES)
        at = (tile // chunk_tiles, tile % chunk_tiles)
        totals = [part[p, k, :, lanes] for k in range(states)]
        upward = even_lanes == (colour == 1)
        slot = [half * there + colour * (1 - there) for there in has]
        for k in range(packs if p == 0 else 0):
            below = halo_x[0, slot[0], at[0], at[1], k]
            above = halo_x[1, slot[1], at[0], at[1], k]
            totals[k] += jnp.where(upward, above, below)
            if k + packs < states:
                totals[k + packs] += pltpu.roll(jnp.where(upward, below, above), cells_y - 1, 0)
        for k in range(states):
            below = halo_y[0, slot[2], p, tile, k]
            above = halo_y[1, slot[3], p, tile, k]
            totals[k] += jnp.where(sub == 0, below, jnp.where(sub == cells_y - 1, above, 0.0))
        return totals

    def half_sweep(colour, half, section):
        other = 1 - colour
        inner_terms(colour, section)
        wait_received(X_WAYS, other, half, 0)
        wait_received(Y_WAYS, other, half, 0)
        if colour == 0 and section == 0:
            @pl.when((half == 0) & at_exit)
            def _():
                pltpu.make_async_copy(table, table, interface_sem.at[0]).wait()

                def lay(k, carry):
                    ids = wanted[k]
                    plane = jnp.zeros((cells_y, cells_z), jnp.float32)
                    for g in range(slots):
                        row = jnp.concatenate([table[g]] * (cells_z // LANES), axis=1)
                        plane = jnp.where(ids == float(g), row, plane)
                    wanted[k] = plane
                    return carry

                lax.fori_loop(0, states, lay, 0)
                for tile in range(tiles):
                    lanes = pl.ds(tile * LANES, LANES)
                    planes = [wanted[k, :, lanes] for k in range(states)]
                    for c in range(2):
                        for k, packed in enumerate(pack_x(planes, even_lanes == (c == 1))[0]):
                            halo_x[1, c, tile // chunk_tiles, tile % chunk_tiles, k] = packed

        if colour == 0 and section == 1:
            @pl.when(half == 0)
            def _():
                pltpu.make_async_copy(arrived, arrived, interface_sem.at[1]).wait()
                row = arrived[0]
                for j in range(1, n_gy):
                    row = row + arrived[j]
                columns = [
                    jnp.sum(
                        jnp.where(lane % BLK == x * cells_y + sub, row, 0.0), axis=1, keepdims=True
                    )
                    for x in range(cells_x)
                ]
                for p in range(pairs):
                    for c in range(2):
                        cell = jnp.where(sub % 2 == c, columns[PLANES[p][0]], columns[PLANES[p][1]])
                        inflow[c, p] = jnp.where(lane == 0, cell, 0.0)

        def update(p, tile):
            lanes = pl.ds(tile * LANES, LANES)
            totals = halo_terms(colour, half, p, tile)
            if section == 0:
                results = [totals[k] * scale[colour, p, k, :, lanes] for k in range(states)]
            else:
                if tile == 0:
                    totals[0] += inflow[colour, p]
                result = None
                for t in range(states):
                    driving = source[colour, p, t, :, lanes] + weights[t] * totals[t]
                    term = matrix[colour, p, t, :, :, lanes] * driving
                    result = term if result is None else result + term
                results = [result[k] for k in range(states)]
            for k in range(states):
                held[colour, p, k, :, lanes] = results[k]
            stage(colour, p, tile, results)

        going_on = pl.when(half < halves - 1)
        for chunk in range(CHUNKS):
            if chunk > 0:
                wait_received(X_WAYS, other, half, chunk)
            for tile in range(chunk * chunk_tiles, (chunk + 1) * chunk_tiles):
                update(0, tile)
            going_on(functools.partial(send, X_WAYS, colour, half + 1, chunk))
        going_on(functools.partial(send, Y_WAYS, colour, half + 1, 0))
        wait_received(Y_WAYS, other, half, 1)
        for tile in range(tiles):
            update(1, tile)
        going_on(functools.partial(send, Y_WAYS, colour, half + 1, 1))

        wait_sent(other, half)

    for section in range(2):
        @pl.when(sa == section)
        def _():
            def sweep(index, carry):
                half_sweep(0, 2 * index, section)
                half_sweep(1, 2 * index + 1, section)
                return carry

            lax.fori_loop(0, SWEEPS, sweep, 0)

    for k in range(states):
        for p in range(pairs):
            first, second = split(held[0, p, k], held[1, p, k])
            out[0, k, PLANES[p][0]] = first
            out[0, k, PLANES[p][1]] = second

    @pl.when(turbine)
    def _():
        for j in range(n_gy):
            inlet_copy(j).wait_send()

    @pl.when(at_exit)
    def _():
        for g in range(slots):
            row_copy(g).wait_send()


def shards(n_gx, n_gy, fields, sources, diagonal, block_inverse, coupling, donors, returns):
    _, states, cells_x, cells_y, cells_z = fields.shape
    pairs = len(PLANES)
    slots = donors.shape[0]
    assert cells_x == 4 and cells_y % 2 == 0 and cells_x * cells_y == BLK
    assert cells_y * cells_z == LANES * BLK and slots == n_gx * n_gy
    f32 = jnp.float32
    block = (states, cells_x, cells_y, cells_z)
    halves = 2 * SWEEPS
    tiles = cells_z // LANES
    packs = (states + 1) // 2
    chunk = (CHUNKS, tiles // CHUNKS)
    hbm = pl.BlockSpec(memory_space=pltpu.HBM)
    vmem = pl.BlockSpec(memory_space=pltpu.VMEM)
    by_colour = (2, pairs, states, cells_y, cells_z)
    return pl.pallas_call(
        functools.partial(kernel, n_gx, n_gy, block),
        out_shape=jax.ShapeDtypeStruct(fields.shape, f32),
        in_specs=[hbm] * 7,
        out_specs=vmem,
        scratch_shapes=[
            pltpu.VMEM(block, f32),
            pltpu.VMEM(block, f32),
            pltpu.VMEM(block, f32),
            pltpu.VMEM((states,) + block, f32),
            pltpu.SMEM(coupling.shape, f32),
            pltpu.SMEM(donors.shape[::-1], jnp.int32),
            pltpu.VMEM(returns.shape, jnp.int32),
            pltpu.VMEM(by_colour, f32),
            pltpu.VMEM(by_colour, f32),
            pltpu.VMEM(by_colour, f32),
            pltpu.VMEM((2, pairs, states, states, cells_y, cells_z), f32),
            pltpu.VMEM(by_colour[1:], f32),
            pltpu.VMEM((2, halves) + chunk + (packs, cells_y, LANES), f32),
            pltpu.VMEM((2, halves, pairs, tiles, states, 1, LANES), f32),
            pltpu.VMEM((2, 2) + chunk + (packs, cells_y, LANES), f32),
            pltpu.VMEM((2, 2, pairs, tiles, states, 1, LANES), f32),
            pltpu.VMEM((2, pairs, cells_y, LANES), f32),
            pltpu.VMEM((states, cells_y, cells_z), f32),
            pltpu.VMEM((slots, 1, LANES), f32),
            pltpu.VMEM((slots, 1, LANES), f32),
            pltpu.VMEM((1, 1, LANES), f32),
            pltpu.VMEM((n_gy, 1, LANES), f32),
            pltpu.SemaphoreType.DMA((7,)),
            pltpu.SemaphoreType.DMA((4, halves, max(CHUNKS, pairs))),
            pltpu.SemaphoreType.DMA((4, halves, max(CHUNKS, pairs))),
            pltpu.SemaphoreType.DMA((slots,)),
            pltpu.SemaphoreType.DMA((2,)),
        ],
        compiler_params=pltpu.CompilerParams(
            collective_id=0, has_side_effects=True, vmem_limit_bytes=60 * 1024 * 1024
        ),
    )(fields, sources, diagonal, block_inverse, coupling, donors.T, returns)


def solution(mesh):
    return jax.shard_map(
        functools.partial(shards, mesh.shape["gx"], mesh.shape["gy"]),
        mesh=mesh,
        in_specs=(
            P("sa", None, "gx", "gy", None),
            P("sa", None, "gx", "gy", None),
            P(None, "gx", "gy", None),
            P(None, None, "gx", "gy", None),
            P(),
            P(),
            P("gy", None),
        ),
        out_specs=P("sa", None, "gx", "gy", None),
        check_vma=False,
    )
```

```python
import functools

import jax
import jax.numpy as jnp
from jax import lax
from jax.experimental import pallas as pl
from jax.experimental.pallas import tpu as pltpu
from jax.sharding import PartitionSpec as P

SWEEPS = 4
BLK = 32
LANES = 128
MESH = pl.DeviceIdType.MESH
CHUNKS = 2
X_WAYS, Y_WAYS = (0, 1), (2, 3)
PLANES = ((0, 3), (2, 1))


def kernel(
    n_gx, n_gy, sizes,
    fields, sources, diagonal, inverse, coupling, donors, returns, out,
    raw, raw_source, raw_diagonal, raw_inverse, weights, list_of, returned,
    held, source, scale, matrix, part,
    halo_x, halo_y, edge_x, edge_y, inflow, wanted, table, rows, inlet, arrived,
    local_sem, send_sem, recv_sem, slot_sem, interface_sem,
):
    states, cells_x, cells_y, cells_z = sizes
    pairs = len(PLANES)
    halves = 2 * SWEEPS
    slots = n_gx * n_gy
    per_row = cells_z // BLK
    packs = (states + 1) // 2
    tiles = cells_z // LANES
    chunk_tiles = tiles // CHUNKS
    gx, gy, sa = lax.axis_index("gx"), lax.axis_index("gy"), lax.axis_index("sa")
    own = gx * n_gy + gy
    has = (
        (gx + n_gx - 1) // n_gx,
        1 - (gx + 1) // n_gx,
        (gy + n_gy - 1) // n_gy,
        1 - (gy + 1) // n_gy,
    )
    peers = ({"gx": gx - 1}, {"gx": gx + 1}, {"gy": gy - 1}, {"gy": gy + 1})
    combustor = sa == 0
    turbine = sa == 1
    at_exit = combustor & (gx == n_gx - 1)

    load_fields = pltpu.make_async_copy(fields.at[0], raw, local_sem.at[0])
    load_source = pltpu.make_async_copy(sources.at[0], raw_source, local_sem.at[1])
    load_diagonal = pltpu.make_async_copy(diagonal, raw_diagonal, local_sem.at[2])
    load_inverse = pltpu.make_async_copy(inverse, raw_inverse, local_sem.at[3])
    load_lists = pltpu.make_async_copy(donors, list_of, local_sem.at[4])
    load_returns = pltpu.make_async_copy(returns, returned, local_sem.at[5])
    load_weights = pltpu.make_async_copy(coupling, weights, local_sem.at[6])
    load_fields.start()
    pl.when(at_exit)(load_lists.start)
    pl.when(at_exit)(load_returns.start)
    load_source.start()
    pl.when(turbine)(load_weights.start)
    pl.when(combustor)(load_diagonal.start)
    pl.when(turbine)(load_inverse.start)

    barrier = pltpu.get_barrier_semaphore()

    def greet(peer):
        pl.semaphore_signal(barrier, inc=1, device_id=peer, device_id_type=MESH)

    for there, peer in zip(has, peers):
        pl.when(there == 1)(functools.partial(greet, peer))

    @pl.when(turbine)
    def _():
        for j in range(n_gy):
            greet({"gx": n_gx - 1, "gy": j, "sa": 0})

    @pl.when(at_exit)
    def _():
        for g in range(slots):
            greet({"gx": g // n_gy, "gy": g % n_gy, "sa": 1})

    sub = lax.broadcasted_iota(jnp.int32, (cells_y, LANES), 0)
    lane = lax.broadcasted_iota(jnp.int32, (cells_y, LANES), 1)
    tall = lax.broadcasted_iota(jnp.int32, (cells_y, cells_z), 0)
    wide = lax.broadcasted_iota(jnp.int32, (cells_y, cells_z), 1)
    parity = (tall + wide) % 2
    even = parity == 0
    even_lanes = (sub + lane) % 2 == 0

    def split(even_plane, odd_plane):
        return (jnp.where(even, even_plane, odd_plane), jnp.where(even, odd_plane, even_plane))

    def split_planes(block, k, p):
        return split(block[k, PLANES[p][0]], block[k, PLANES[p][1]])

    def pack_x(values, *choices):
        moved = [pltpu.roll(values[k], 1, 0) for k in range(packs, states)]
        moved += [values[k] for k in range(states - packs, packs)]
        return [
            [jnp.where(chosen, values[k], moved[k]) for k in range(packs)] for chosen in choices
        ]

    def stage(colour, p, tile, values):
        if p == 0:
            faces = pack_x(values, even_lanes == (colour == 0), even_lanes == (colour == 1))
            for way in range(2):
                for k in range(packs):
                    at = (tile // chunk_tiles, tile % chunk_tiles)
                    edge_x[way, colour, at[0], at[1], k] = faces[way][k]
        for k in range(states):
            edge_y[0, colour, p, tile, k] = values[k][0:1]
            edge_y[1, colour, p, tile, k] = values[k][cells_y - 1 : cells_y]

    def halo_copy(way, colour, half, piece):
        edges, halos = (edge_x, halo_x) if way < 2 else (edge_y, halo_y)
        return pltpu.make_async_remote_copy(
            src_ref=edges.at[way % 2, colour, piece],
            dst_ref=halos.at[1 - way % 2, half, piece],
            send_sem=send_sem.at[way, half, piece],
            recv_sem=recv_sem.at[way, half, piece],
            device_id=peers[way],
            device_id_type=MESH,
        )

    def send(ways, colour, half, piece):
        for way in ways:
            pl.when(has[way] == 1)(lambda way=way: halo_copy(way, colour, half, piece).start())

    def wait_sent(colour, half):
        for way in range(4):
            @pl.when(has[way] == 1)
            def _():
                for piece in range(CHUNKS if way < 2 else pairs):
                    halo_copy(way, colour, half, piece).wait_send()

    def wait_received(ways, colour, half, piece):
        for way in ways:
            pl.when(has[way] == 1)(
                lambda way=way: halo_copy(way ^ 1, colour, half, piece).wait_recv()
            )

    def inlet_copy(j):
        return pltpu.make_async_remote_copy(
            src_ref=inlet.at[0],
            dst_ref=table.at[own],
            send_sem=slot_sem.at[j],
            recv_sem=interface_sem.at[0],
            device_id={"gx": n_gx - 1, "gy": j, "sa": 0},
            device_id_type=MESH,
        )

    def row_copy(g):
        return pltpu.make_async_remote_copy(
            src_ref=rows.at[g],
            dst_ref=arrived.at[gy],
            send_sem=slot_sem.at[g],
            recv_sem=interface_sem.at[1],
            device_id={"gx": g // n_gy, "gy": g % n_gy, "sa": 1},
            device_id_type=MESH,
        )

    @pl.when(has[0] == 0)
    def _():
        halo_x[0, 0:2] = jnp.zeros((2,) + halo_x.shape[2:], jnp.float32)

    @pl.when((has[1] == 0) & turbine)
    def _():
        halo_x[1, 0:2] = jnp.zeros((2,) + halo_x.shape[2:], jnp.float32)

    for side in range(2):
        @pl.when(has[2 + side] == 0)
        def _():
            halo_y[side, 0:2] = jnp.zeros((2,) + halo_y.shape[2:], jnp.float32)

    load_fields.wait()
    for k in range(states):
        for p in range(pairs):
            held[0, p, k], held[1, p, k] = split_planes(raw, k, p)
    for tile in range(tiles):
        lanes = pl.ds(tile * LANES, LANES)
        for p in range(pairs):
            stage(1, p, tile, [held[1, p, k, :, lanes] for k in range(states)])

    @pl.when(turbine)
    def _():
        row = jnp.zeros((cells_y, LANES), jnp.float32)
        for x in range(cells_x):
            row = jnp.where(lane % BLK == x * cells_y + sub, raw[0, x, :, 0:1], row)
        inlet[0] = jnp.sum(row, axis=0, keepdims=True)

    @pl.when(at_exit)
    def _():
        load_lists.wait()
        slot_row = lax.broadcasted_iota(jnp.int32, (slots, LANES), 0)
        in_state = tall * per_row + wide // BLK

        def take(e, total):
            block = jnp.where(list_of[0, e] == gy, list_of[1, e], -1)
            found = jnp.zeros((cells_y, cells_z), jnp.float32)
            for k in range(states):
                here = in_state == block - k * (cells_y * per_row)
                found = jnp.where(here, raw[k, cells_x - 1], found)
            row = jnp.sum(found, axis=0, keepdims=True)
            row = sum(row[:, i * LANES : (i + 1) * LANES] for i in range(cells_z // LANES))
            return jnp.where(slot_row == list_of[2, e], row, total)

        total = lax.fori_loop(0, slots, take, jnp.zeros((slots, LANES), jnp.float32), unroll=4)
        for g in range(slots):
            rows[g] = total[g : g + 1]

    met = has[0] + has[1] + has[2] + has[3] + sa * n_gy + (1 - sa) * (1 - has[1]) * slots
    pl.semaphore_wait(barrier, met)
    for chunk in range(CHUNKS):
        send(X_WAYS, 1, 0, chunk)
    for p in range(pairs):
        send(Y_WAYS, 1, 0, p)

    @pl.when(turbine)
    def _():
        for j in range(n_gy):
            inlet_copy(j).start()

    @pl.when(at_exit)
    def _():
        for g in range(slots):
            row_copy(g).start()

        spread_from = lax.broadcasted_iota(jnp.int32, (LANES, cells_z), 0) % per_row
        spread_to = lax.broadcasted_iota(jnp.int32, (LANES, cells_z), 1) // BLK
        spread = jnp.where(spread_from == spread_to, 1.0, 0.0)
        load_returns.wait()
        for k in range(states):
            ids = returned[0:1, k * LANES : (k + 1) * LANES].astype(jnp.float32)
            ids = jnp.where(lane // per_row == sub, ids, 0.0)
            wanted[k] = jnp.dot(
                ids, spread, preferred_element_type=jnp.float32
            )

    load_source.wait()
    for k in range(states):
        for p in range(pairs):
            source[0, p, k], source[1, p, k] = split_planes(raw_source, k, p)

    @pl.when(combustor)
    def _():
        load_diagonal.wait()
        for k in range(states):
            for p in range(pairs):
                first, second = split_planes(raw_diagonal, k, p)
                scale[0, p, k] = 1.0 / (6.0 + first)
                scale[1, p, k] = 1.0 / (6.0 + second)

    @pl.when(turbine)
    def _():
        load_weights.wait()
        load_inverse.wait()

        def pack(s, carry):
            for t in range(states):
                for p in range(pairs):
                    first, second = split_planes(raw_inverse.at[s], t, p)
                    matrix[0, p, t, s] = first
                    matrix[1, p, t, s] = second
            return carry

        lax.fori_loop(0, states, pack, 0)

    def inner_terms(colour, section):
        other = 1 - colour
        for p in range(pairs):
            values = [held[other, p, k] for k in range(states)]
            lower = [pltpu.roll(value, 1, 1) for value in values]
            upper = [pltpu.roll(value, cells_z - 1, 1) for value in values]
            for k in range(states):
                if section == 0:
                    before = lower[k - 1] if k > 0 else 0.0
                    after = upper[k + 1] if k < states - 1 else 0.0
                else:
                    before = held[colour, p, k, :, 0:1] if k > 0 else 0.0
                    after = 0.0
                total = held[other, 1, k]
                if p == 1:
                    total += held[other, 0, k]
                total += jnp.where(wide == 0, before, lower[k])
                total += jnp.where(wide == cells_z - 1, after, upper[k])
                total += jnp.where(tall == 0, 0.0, pltpu.roll(values[k], 1, 0))
                total += jnp.where(tall == cells_y - 1, 0.0, pltpu.roll(values[k], cells_y - 1, 0))
                if section == 0:
                    total += source[colour, p, k]
                part[p, k] = total

    def halo_terms(colour, half, p, tile):
        lanes = pl.ds(tile * LANES, LANES)
        at = (tile // chunk_tiles, tile % chunk_tiles)
        totals = [part[p, k, :, lanes] for k in range(states)]
        upward = even_lanes == (colour == 1)
        slot = [half * there + colour * (1 - there) for there in has]
        for k in range(packs if p == 0 else 0):
            below = halo_x[0, slot[0], at[0], at[1], k]
            above = halo_x[1, slot[1], at[0], at[1], k]
            totals[k] += jnp.where(upward, above, below)
            if k + packs < states:
                totals[k + packs] += pltpu.roll(jnp.where(upward, below, above), cells_y - 1, 0)
        for k in range(states):
            below = halo_y[0, slot[2], p, tile, k]
            above = halo_y[1, slot[3], p, tile, k]
            totals[k] += jnp.where(sub == 0, below, jnp.where(sub == cells_y - 1, above, 0.0))
        return totals

    def half_sweep(colour, half, section):
        other = 1 - colour
        inner_terms(colour, section)
        wait_received(X_WAYS, other, half, 0)
        wait_received(Y_WAYS, other, half, 0)
        if colour == 0 and section == 0:
            @pl.when((half == 0) & at_exit)
            def _():
                pltpu.make_async_copy(table, table, interface_sem.at[0]).wait()

                def lay(k, carry):
                    ids = wanted[k]
                    plane = jnp.zeros((cells_y, cells_z), jnp.float32)
                    for g in range(slots):
                        row = jnp.concatenate([table[g]] * (cells_z // LANES), axis=1)
                        plane = jnp.where(ids == float(g), row, plane)
                    wanted[k] = plane
                    return carry

                lax.fori_loop(0, states, lay, 0)
                for tile in range(tiles):
                    lanes = pl.ds(tile * LANES, LANES)
                    planes = [wanted[k, :, lanes] for k in range(states)]
                    for c in range(2):
                        for k, packed in enumerate(pack_x(planes, even_lanes == (c == 1))[0]):
                            halo_x[1, c, tile // chunk_tiles, tile % chunk_tiles, k] = packed

        if colour == 0 and section == 1:
            @pl.when(half == 0)
            def _():
                pltpu.make_async_copy(arrived, arrived, interface_sem.at[1]).wait()
                row = arrived[0]
                for j in range(1, n_gy):
                    row = row + arrived[j]
                columns = [
                    jnp.sum(
                        jnp.where(lane % BLK == x * cells_y + sub, row, 0.0), axis=1, keepdims=True
                    )
                    for x in range(cells_x)
                ]
                for p in range(pairs):
                    for c in range(2):
                        cell = jnp.where(sub % 2 == c, columns[PLANES[p][0]], columns[PLANES[p][1]])
                        inflow[c, p] = jnp.where(lane == 0, cell, 0.0)

        def update(p, tile):
            lanes = pl.ds(tile * LANES, LANES)
            totals = halo_terms(colour, half, p, tile)
            if section == 0:
                results = [totals[k] * scale[colour, p, k, :, lanes] for k in range(states)]
            else:
                if tile == 0:
                    totals[0] += inflow[colour, p]
                result = None
                for t in range(states):
                    driving = source[colour, p, t, :, lanes] + weights[t] * totals[t]
                    term = matrix[colour, p, t, :, :, lanes] * driving
                    result = term if result is None else result + term
                results = [result[k] for k in range(states)]
            for k in range(states):
                held[colour, p, k, :, lanes] = results[k]
            stage(colour, p, tile, results)

        going_on = pl.when(half < halves - 1)
        for chunk in range(CHUNKS):
            if chunk > 0:
                wait_received(X_WAYS, other, half, chunk)
            for tile in range(chunk * chunk_tiles, (chunk + 1) * chunk_tiles):
                update(0, tile)
            going_on(functools.partial(send, X_WAYS, colour, half + 1, chunk))
        going_on(functools.partial(send, Y_WAYS, colour, half + 1, 0))
        wait_received(Y_WAYS, other, half, 1)
        for tile in range(tiles):
            update(1, tile)
        going_on(functools.partial(send, Y_WAYS, colour, half + 1, 1))

        wait_sent(other, half)

    for section in range(2):
        @pl.when(sa == section)
        def _():
            def sweep(index, carry):
                half_sweep(0, 2 * index, section)
                half_sweep(1, 2 * index + 1, section)
                return carry

            lax.fori_loop(0, SWEEPS, sweep, 0)

    for k in range(states):
        for p in range(pairs):
            first, second = split(held[0, p, k], held[1, p, k])
            out[0, k, PLANES[p][0]] = first
            out[0, k, PLANES[p][1]] = second

    @pl.when(turbine)
    def _():
        for j in range(n_gy):
            inlet_copy(j).wait_send()

    @pl.when(at_exit)
    def _():
        for g in range(slots):
            row_copy(g).wait_send()


def shards(n_gx, n_gy, fields, sources, diagonal, block_inverse, coupling, donors, returns):
    _, states, cells_x, cells_y, cells_z = fields.shape
    pairs = len(PLANES)
    slots = donors.shape[0]
    assert cells_x == 4 and cells_y % 2 == 0 and cells_x * cells_y == BLK
    assert cells_y * cells_z == LANES * BLK and slots == n_gx * n_gy
    f32 = jnp.float32
    block = (states, cells_x, cells_y, cells_z)
    halves = 2 * SWEEPS
    tiles = cells_z // LANES
    packs = (states + 1) // 2
    chunk = (CHUNKS, tiles // CHUNKS)
    operands = [
        pltpu.with_memory_space_constraint(operand, pltpu.HBM)
        for operand in (fields, sources, diagonal, block_inverse, coupling, donors.T, returns)
    ]
    hbm = pl.BlockSpec(memory_space=pltpu.HBM)
    vmem = pl.BlockSpec(memory_space=pltpu.VMEM)
    by_colour = (2, pairs, states, cells_y, cells_z)
    return pl.pallas_call(
        functools.partial(kernel, n_gx, n_gy, block),
        out_shape=jax.ShapeDtypeStruct(fields.shape, f32),
        in_specs=[hbm] * 7,
        out_specs=vmem,
        scratch_shapes=[
            pltpu.VMEM(block, f32),
            pltpu.VMEM(block, f32),
            pltpu.VMEM(block, f32),
            pltpu.VMEM((states,) + block, f32),
            pltpu.SMEM(coupling.shape, f32),
            pltpu.SMEM(donors.shape[::-1], jnp.int32),
            pltpu.VMEM(returns.shape, jnp.int32),
            pltpu.VMEM(by_colour, f32),
            pltpu.VMEM(by_colour, f32),
            pltpu.VMEM(by_colour, f32),
            pltpu.VMEM((2, pairs, states, states, cells_y, cells_z), f32),
            pltpu.VMEM(by_colour[1:], f32),
            pltpu.VMEM((2, halves) + chunk + (packs, cells_y, LANES), f32),
            pltpu.VMEM((2, halves, pairs, tiles, states, 1, LANES), f32),
            pltpu.VMEM((2, 2) + chunk + (packs, cells_y, LANES), f32),
            pltpu.VMEM((2, 2, pairs, tiles, states, 1, LANES), f32),
            pltpu.VMEM((2, pairs, cells_y, LANES), f32),
            pltpu.VMEM((states, cells_y, cells_z), f32),
            pltpu.VMEM((slots, 1, LANES), f32),
            pltpu.VMEM((slots, 1, LANES), f32),
            pltpu.VMEM((1, 1, LANES), f32),
            pltpu.VMEM((n_gy, 1, LANES), f32),
            pltpu.SemaphoreType.DMA((7,)),
            pltpu.SemaphoreType.DMA((4, halves, max(CHUNKS, pairs))),
            pltpu.SemaphoreType.DMA((4, halves, max(CHUNKS, pairs))),
            pltpu.SemaphoreType.DMA((slots,)),
            pltpu.SemaphoreType.DMA((2,)),
        ],
        compiler_params=pltpu.CompilerParams(
            collective_id=0, has_side_effects=True, vmem_limit_bytes=32 * 1024 * 1024
        ),
    )(*operands)


def solution(mesh):
    return jax.shard_map(
        functools.partial(shards, mesh.shape["gx"], mesh.shape["gy"]),
        mesh=mesh,
        in_specs=(
            P("sa", None, "gx", "gy", None),
            P("sa", None, "gx", "gy", None),
            P(None, "gx", "gy", None),
            P(None, None, "gx", "gy", None),
            P(),
            P(),
            P("gy", None),
        ),
        out_specs=P("sa", None, "gx", "gy", None),
        check_vma=False,
    )
```

```python
import functools

import jax
import jax.numpy as jnp
from jax import lax
from jax.experimental import pallas as pl
from jax.experimental.pallas import tpu as pltpu
from jax.sharding import PartitionSpec as P

SWEEPS = 4
BLK = 32
LANES = 128
MESH = pl.DeviceIdType.MESH
CHUNKS = 1
X_WAYS, Y_WAYS = (0, 1), (2, 3)
PLANES = ((0, 3), (2, 1))


def kernel(
    n_gx, n_gy, sizes,
    fields, sources, diagonal, inverse, coupling, donors, returns, out,
    raw, raw_source, raw_diagonal, raw_inverse, weights, list_of, returned,
    held, source, scale, matrix, part,
    halo_x, halo_y, edge_x, edge_y, inflow, wanted, table, rows, inlet, arrived,
    local_sem, send_sem, recv_sem, slot_sem, interface_sem,
):
    states, cells_x, cells_y, cells_z = sizes
    pairs = len(PLANES)
    halves = 2 * SWEEPS
    slots = n_gx * n_gy
    per_row = cells_z // BLK
    packs = (states + 1) // 2
    tiles = cells_z // LANES
    chunk_tiles = tiles // CHUNKS
    gx, gy, sa = lax.axis_index("gx"), lax.axis_index("gy"), lax.axis_index("sa")
    own = gx * n_gy + gy
    has = (
        (gx + n_gx - 1) // n_gx,
        1 - (gx + 1) // n_gx,
        (gy + n_gy - 1) // n_gy,
        1 - (gy + 1) // n_gy,
    )
    peers = ({"gx": gx - 1}, {"gx": gx + 1}, {"gy": gy - 1}, {"gy": gy + 1})
    combustor = sa == 0
    turbine = sa == 1
    at_exit = combustor & (gx == n_gx - 1)

    load_fields = pltpu.make_async_copy(fields.at[0], raw, local_sem.at[0])
    load_source = pltpu.make_async_copy(sources.at[0], raw_source, local_sem.at[1])
    load_diagonal = pltpu.make_async_copy(diagonal, raw_diagonal, local_sem.at[2])
    load_inverse = pltpu.make_async_copy(inverse, raw_inverse, local_sem.at[3])
    load_lists = pltpu.make_async_copy(donors, list_of, local_sem.at[4])
    load_returns = pltpu.make_async_copy(returns, returned, local_sem.at[5])
    load_weights = pltpu.make_async_copy(coupling, weights, local_sem.at[6])
    load_fields.start()
    pl.when(at_exit)(load_lists.start)
    pl.when(at_exit)(load_returns.start)
    load_source.start()
    pl.when(turbine)(load_weights.start)
    pl.when(combustor)(load_diagonal.start)
    pl.when(turbine)(load_inverse.start)

    barrier = pltpu.get_barrier_semaphore()

    def greet(peer):
        pl.semaphore_signal(barrier, inc=1, device_id=peer, device_id_type=MESH)

    for there, peer in zip(has, peers):
        pl.when(there == 1)(functools.partial(greet, peer))

    @pl.when(turbine)
    def _():
        for j in range(n_gy):
            greet({"gx": n_gx - 1, "gy": j, "sa": 0})

    @pl.when(at_exit)
    def _():
        for g in range(slots):
            greet({"gx": g // n_gy, "gy": g % n_gy, "sa": 1})

    sub = lax.broadcasted_iota(jnp.int32, (cells_y, LANES), 0)
    lane = lax.broadcasted_iota(jnp.int32, (cells_y, LANES), 1)
    tall = lax.broadcasted_iota(jnp.int32, (cells_y, cells_z), 0)
    wide = lax.broadcasted_iota(jnp.int32, (cells_y, cells_z), 1)
    parity = (tall + wide) % 2
    even = parity == 0
    even_lanes = (sub + lane) % 2 == 0

    def split(even_plane, odd_plane):
        return (jnp.where(even, even_plane, odd_plane), jnp.where(even, odd_plane, even_plane))

    def split_planes(block, k, p):
        return split(block[k, PLANES[p][0]], block[k, PLANES[p][1]])

    def pack_x(values, *choices):
        moved = [pltpu.roll(values[k], 1, 0) for k in range(packs, states)]
        moved += [values[k] for k in range(states - packs, packs)]
        return [
            [jnp.where(chosen, values[k], moved[k]) for k in range(packs)] for chosen in choices
        ]

    def stage(colour, p, tile, values):
        if p == 0:
            faces = pack_x(values, even_lanes == (colour == 0), even_lanes == (colour == 1))
            for way in range(2):
                for k in range(packs):
                    at = (tile // chunk_tiles, tile % chunk_tiles)
                    edge_x[way, colour, at[0], at[1], k] = faces[way][k]
        for k in range(states):
            edge_y[0, colour, p, tile, k] = values[k][0:1]
            edge_y[1, colour, p, tile, k] = values[k][cells_y - 1 : cells_y]

    def halo_copy(way, colour, half, piece):
        edges, halos = (edge_x, halo_x) if way < 2 else (edge_y, halo_y)
        return pltpu.make_async_remote_copy(
            src_ref=edges.at[way % 2, colour, piece],
            dst_ref=halos.at[1 - way % 2, half, piece],
            send_sem=send_sem.at[way, half, piece],
            recv_sem=recv_sem.at[way, half, piece],
            device_id=peers[way],
            device_id_type=MESH,
        )

    def send(ways, colour, half, piece):
        for way in ways:
            pl.when(has[way] == 1)(lambda way=way: halo_copy(way, colour, half, piece).start())

    def wait_sent(colour, half):
        for way in range(4):
            @pl.when(has[way] == 1)
            def _():
                for piece in range(CHUNKS if way < 2 else pairs):
                    halo_copy(way, colour, half, piece).wait_send()

    def wait_received(ways, colour, half, piece):
        for way in ways:
            pl.when(has[way] == 1)(
                lambda way=way: halo_copy(way ^ 1, colour, half, piece).wait_recv()
            )

    def inlet_copy(j):
        return pltpu.make_async_remote_copy(
            src_ref=inlet.at[0],
            dst_ref=table.at[own],
            send_sem=slot_sem.at[j],
            recv_sem=interface_sem.at[0],
            device_id={"gx": n_gx - 1, "gy": j, "sa": 0},
            device_id_type=MESH,
        )

    def row_copy(g):
        return pltpu.make_async_remote_copy(
            src_ref=rows.at[g],
            dst_ref=arrived.at[gy],
            send_sem=slot_sem.at[g],
            recv_sem=interface_sem.at[1],
            device_id={"gx": g // n_gy, "gy": g % n_gy, "sa": 1},
            device_id_type=MESH,
        )

    @pl.when(has[0] == 0)
    def _():
        halo_x[0, 0:2] = jnp.zeros((2,) + halo_x.shape[2:], jnp.float32)

    @pl.when((has[1] == 0) & turbine)
    def _():
        halo_x[1, 0:2] = jnp.zeros((2,) + halo_x.shape[2:], jnp.float32)

    for side in range(2):
        @pl.when(has[2 + side] == 0)
        def _():
            halo_y[side, 0:2] = jnp.zeros((2,) + halo_y.shape[2:], jnp.float32)

    load_fields.wait()
    for k in range(states):
        for p in range(pairs):
            held[0, p, k], held[1, p, k] = split_planes(raw, k, p)
    for tile in range(tiles):
        lanes = pl.ds(tile * LANES, LANES)
        for p in range(pairs):
            stage(1, p, tile, [held[1, p, k, :, lanes] for k in range(states)])

    @pl.when(turbine)
    def _():
        row = jnp.zeros((cells_y, LANES), jnp.float32)
        for x in range(cells_x):
            row = jnp.where(lane % BLK == x * cells_y + sub, raw[0, x, :, 0:1], row)
        inlet[0] = jnp.sum(row, axis=0, keepdims=True)

    @pl.when(at_exit)
    def _():
        load_lists.wait()
        slot_row = lax.broadcasted_iota(jnp.int32, (slots, LANES), 0)
        in_state = tall * per_row + wide // BLK

        def take(e, total):
            block = jnp.where(list_of[0, e] == gy, list_of[1, e], -1)
            found = jnp.zeros((cells_y, cells_z), jnp.float32)
            for k in range(states):
                here = in_state == block - k * (cells_y * per_row)
                found = jnp.where(here, raw[k, cells_x - 1], found)
            row = jnp.sum(found, axis=0, keepdims=True)
            row = sum(row[:, i * LANES : (i + 1) * LANES] for i in range(cells_z // LANES))
            return jnp.where(slot_row == list_of[2, e], row, total)

        total = lax.fori_loop(0, slots, take, jnp.zeros((slots, LANES), jnp.float32), unroll=4)
        for g in range(slots):
            rows[g] = total[g : g + 1]

    met = has[0] + has[1] + has[2] + has[3] + sa * n_gy + (1 - sa) * (1 - has[1]) * slots
    pl.semaphore_wait(barrier, met)
    for p in range(pairs):
        send(Y_WAYS, 1, 0, p)
    for chunk in range(CHUNKS):
        send(X_WAYS, 1, 0, chunk)

    @pl.when(turbine)
    def _():
        for j in range(n_gy):
            inlet_copy(j).start()

    @pl.when(at_exit)
    def _():
        for g in range(slots):
            row_copy(g).start()

        spread_from = lax.broadcasted_iota(jnp.int32, (LANES, cells_z), 0) % per_row
        spread_to = lax.broadcasted_iota(jnp.int32, (LANES, cells_z), 1) // BLK
        spread = jnp.where(spread_from == spread_to, 1.0, 0.0)
        load_returns.wait()
        for k in range(states):
            ids = returned[0:1, k * LANES : (k + 1) * LANES].astype(jnp.float32)
            ids = jnp.where(lane // per_row == sub, ids, 0.0)
            wanted[k] = jnp.dot(
                ids, spread, preferred_element_type=jnp.float32
            )

    load_source.wait()
    for k in range(states):
        for p in range(pairs):
            source[0, p, k], source[1, p, k] = split_planes(raw_source, k, p)

    @pl.when(combustor)
    def _():
        load_diagonal.wait()
        for k in range(states):
            for p in range(pairs):
                first, second = split_planes(raw_diagonal, k, p)
                scale[0, p, k] = 1.0 / (6.0 + first)
                scale[1, p, k] = 1.0 / (6.0 + second)

    @pl.when(turbine)
    def _():
        load_weights.wait()
        load_inverse.wait()

        def pack(s, carry):
            for t in range(states):
                for p in range(pairs):
                    first, second = split_planes(raw_inverse.at[s], t, p)
                    matrix[0, p, t, s] = first
                    matrix[1, p, t, s] = second
            return carry

        lax.fori_loop(0, states, pack, 0)

    def inner_terms(colour, section):
        other = 1 - colour
        for p in range(pairs):
            values = [held[other, p, k] for k in range(states)]
            lower = [pltpu.roll(value, 1, 1) for value in values]
            upper = [pltpu.roll(value, cells_z - 1, 1) for value in values]
            for k in range(states):
                if section == 0:
                    before = lower[k - 1] if k > 0 else 0.0
                    after = upper[k + 1] if k < states - 1 else 0.0
                else:
                    before = held[colour, p, k, :, 0:1] if k > 0 else 0.0
                    after = 0.0
                total = held[other, 1, k]
                if p == 1:
                    total += held[other, 0, k]
                total += jnp.where(wide == 0, before, lower[k])
                total += jnp.where(wide == cells_z - 1, after, upper[k])
                total += jnp.where(tall == 0, 0.0, pltpu.roll(values[k], 1, 0))
                total += jnp.where(tall == cells_y - 1, 0.0, pltpu.roll(values[k], cells_y - 1, 0))
                if section == 0:
                    total += source[colour, p, k]
                part[p, k] = total

    def halo_terms(colour, half, p, tile):
        lanes = pl.ds(tile * LANES, LANES)
        at = (tile // chunk_tiles, tile % chunk_tiles)
        totals = [part[p, k, :, lanes] for k in range(states)]
        upward = even_lanes == (colour == 1)
        slot = [half * there + colour * (1 - there) for there in has]
        for k in range(packs if p == 0 else 0):
            below = halo_x[0, slot[0], at[0], at[1], k]
            above = halo_x[1, slot[1], at[0], at[1], k]
            totals[k] += jnp.where(upward, above, below)
            if k + packs < states:
                totals[k + packs] += pltpu.roll(jnp.where(upward, below, above), cells_y - 1, 0)
        for k in range(states):
            below = halo_y[0, slot[2], p, tile, k]
            above = halo_y[1, slot[3], p, tile, k]
            totals[k] += jnp.where(sub == 0, below, jnp.where(sub == cells_y - 1, above, 0.0))
        return totals

    def half_sweep(colour, half, section):
        other = 1 - colour
        inner_terms(colour, section)
        wait_received(X_WAYS, other, half, 0)
        wait_received(Y_WAYS, other, half, 0)
        if colour == 0 and section == 0:
            @pl.when((half == 0) & at_exit)
            def _():
                pltpu.make_async_copy(table, table, interface_sem.at[0]).wait()

                def lay(k, carry):
                    ids = wanted[k]
                    plane = jnp.zeros((cells_y, cells_z), jnp.float32)
                    for g in range(slots):
                        row = jnp.concatenate([table[g]] * (cells_z // LANES), axis=1)
                        plane = jnp.where(ids == float(g), row, plane)
                    wanted[k] = plane
                    return carry

                lax.fori_loop(0, states, lay, 0)
                for tile in range(tiles):
                    lanes = pl.ds(tile * LANES, LANES)
                    planes = [wanted[k, :, lanes] for k in range(states)]
                    for c in range(2):
                        for k, packed in enumerate(pack_x(planes, even_lanes == (c == 1))[0]):
                            halo_x[1, c, tile // chunk_tiles, tile % chunk_tiles, k] = packed

        if colour == 0 and section == 1:
            @pl.when(half == 0)
            def _():
                pltpu.make_async_copy(arrived, arrived, interface_sem.at[1]).wait()
                row = arrived[0]
                for j in range(1, n_gy):
                    row = row + arrived[j]
                columns = [
                    jnp.sum(
                        jnp.where(lane % BLK == x * cells_y + sub, row, 0.0), axis=1, keepdims=True
                    )
                    for x in range(cells_x)
                ]
                for p in range(pairs):
                    for c in range(2):
                        cell = jnp.where(sub % 2 == c, columns[PLANES[p][0]], columns[PLANES[p][1]])
                        inflow[c, p] = jnp.where(lane == 0, cell, 0.0)

        def update(p, tile):
            lanes = pl.ds(tile * LANES, LANES)
            totals = halo_terms(colour, half, p, tile)
            if section == 0:
                results = [totals[k] * scale[colour, p, k, :, lanes] for k in range(states)]
            else:
                if tile == 0:
                    totals[0] += inflow[colour, p]
                result = None
                for t in range(states):
                    driving = source[colour, p, t, :, lanes] + weights[t] * totals[t]
                    term = matrix[colour, p, t, :, :, lanes] * driving
                    result = term if result is None else result + term
                results = [result[k] for k in range(states)]
            for k in range(states):
                held[colour, p, k, :, lanes] = results[k]
            stage(colour, p, tile, results)

        going_on = pl.when(half < halves - 1)
        for chunk in range(CHUNKS):
            if chunk > 0:
                wait_received(X_WAYS, other, half, chunk)
            for tile in range(chunk * chunk_tiles, (chunk + 1) * chunk_tiles):
                update(0, tile)
            if chunk == CHUNKS - 1:
                going_on(functools.partial(send, Y_WAYS, colour, half + 1, 0))
            going_on(functools.partial(send, X_WAYS, colour, half + 1, chunk))
        wait_received(Y_WAYS, other, half, 1)
        for tile in range(tiles):
            update(1, tile)
        going_on(functools.partial(send, Y_WAYS, colour, half + 1, 1))

        wait_sent(other, half)

    for section in range(2):
        @pl.when(sa == section)
        def _():
            def sweep(index, carry):
                half_sweep(0, 2 * index, section)
                half_sweep(1, 2 * index + 1, section)
                return carry

            lax.fori_loop(0, SWEEPS, sweep, 0)

    for k in range(states):
        for p in range(pairs):
            first, second = split(held[0, p, k], held[1, p, k])
            out[0, k, PLANES[p][0]] = first
            out[0, k, PLANES[p][1]] = second

    @pl.when(turbine)
    def _():
        for j in range(n_gy):
            inlet_copy(j).wait_send()

    @pl.when(at_exit)
    def _():
        for g in range(slots):
            row_copy(g).wait_send()


def shards(n_gx, n_gy, fields, sources, diagonal, block_inverse, coupling, donors, returns):
    _, states, cells_x, cells_y, cells_z = fields.shape
    pairs = len(PLANES)
    slots = donors.shape[0]
    assert cells_x == 4 and cells_y % 2 == 0 and cells_x * cells_y == BLK
    assert cells_y * cells_z == LANES * BLK and slots == n_gx * n_gy
    f32 = jnp.float32
    block = (states, cells_x, cells_y, cells_z)
    halves = 2 * SWEEPS
    tiles = cells_z // LANES
    packs = (states + 1) // 2
    chunk = (CHUNKS, tiles // CHUNKS)
    operands = [
        pltpu.with_memory_space_constraint(operand, pltpu.HBM)
        for operand in (fields, sources, diagonal, block_inverse, coupling, donors.T, returns)
    ]
    hbm = pl.BlockSpec(memory_space=pltpu.HBM)
    vmem = pl.BlockSpec(memory_space=pltpu.VMEM)
    by_colour = (2, pairs, states, cells_y, cells_z)
    return pl.pallas_call(
        functools.partial(kernel, n_gx, n_gy, block),
        out_shape=jax.ShapeDtypeStruct(fields.shape, f32),
        in_specs=[hbm] * 7,
        out_specs=vmem,
        scratch_shapes=[
            pltpu.VMEM(block, f32),
            pltpu.VMEM(block, f32),
            pltpu.VMEM(block, f32),
            pltpu.VMEM((states,) + block, f32),
            pltpu.SMEM(coupling.shape, f32),
            pltpu.SMEM(donors.shape[::-1], jnp.int32),
            pltpu.VMEM(returns.shape, jnp.int32),
            pltpu.VMEM(by_colour, f32),
            pltpu.VMEM(by_colour, f32),
            pltpu.VMEM(by_colour, f32),
            pltpu.VMEM((2, pairs, states, states, cells_y, cells_z), f32),
            pltpu.VMEM(by_colour[1:], f32),
            pltpu.VMEM((2, halves) + chunk + (packs, cells_y, LANES), f32),
            pltpu.VMEM((2, halves, pairs, tiles, states, 1, LANES), f32),
            pltpu.VMEM((2, 2) + chunk + (packs, cells_y, LANES), f32),
            pltpu.VMEM((2, 2, pairs, tiles, states, 1, LANES), f32),
            pltpu.VMEM((2, pairs, cells_y, LANES), f32),
            pltpu.VMEM((states, cells_y, cells_z), f32),
            pltpu.VMEM((slots, 1, LANES), f32),
            pltpu.VMEM((slots, 1, LANES), f32),
            pltpu.VMEM((1, 1, LANES), f32),
            pltpu.VMEM((n_gy, 1, LANES), f32),
            pltpu.SemaphoreType.DMA((7,)),
            pltpu.SemaphoreType.DMA((4, halves, max(CHUNKS, pairs))),
            pltpu.SemaphoreType.DMA((4, halves, max(CHUNKS, pairs))),
            pltpu.SemaphoreType.DMA((slots,)),
            pltpu.SemaphoreType.DMA((2,)),
        ],
        compiler_params=pltpu.CompilerParams(
            collective_id=0, has_side_effects=True, vmem_limit_bytes=32 * 1024 * 1024
        ),
    )(*operands)


def solution(mesh):
    return jax.shard_map(
        functools.partial(shards, mesh.shape["gx"], mesh.shape["gy"]),
        mesh=mesh,
        in_specs=(
            P("sa", None, "gx", "gy", None),
            P("sa", None, "gx", "gy", None),
            P(None, "gx", "gy", None),
            P(None, None, "gx", "gy", None),
            P(),
            P(),
            P("gy", None),
        ),
        out_specs=P("sa", None, "gx", "gy", None),
        check_vma=False,
    )
```

```python
import functools

import jax
import jax.numpy as jnp
from jax import lax
from jax.experimental import pallas as pl
from jax.experimental.pallas import tpu as pltpu
from jax.sharding import PartitionSpec as P

SWEEPS = 4
BLK = 32
LANES = 128
MESH = pl.DeviceIdType.MESH
CHUNKS = 2
X_WAYS, Y_WAYS = (0, 1), (2, 3)
PLANES = ((0, 3), (2, 1))


def kernel(
    n_gx, n_gy, sizes,
    fields, sources, diagonal, inverse, coupling, donors, returns, out,
    raw, raw_source, raw_diagonal, raw_inverse, weights, list_of, returned,
    held, source, scale, matrix, part,
    halo_x, halo_y, edge_x, edge_y, inflow, wanted, table, rows, inlet, arrived,
    local_sem, send_sem, recv_sem, slot_sem, interface_sem,
):
    states, cells_x, cells_y, cells_z = sizes
    pairs = len(PLANES)
    halves = 2 * SWEEPS
    slots = n_gx * n_gy
    per_row = cells_z // BLK
    packs = (states + 1) // 2
    tiles = cells_z // LANES
    chunk_tiles = tiles // CHUNKS
    gx, gy, sa = lax.axis_index("gx"), lax.axis_index("gy"), lax.axis_index("sa")
    own = gx * n_gy + gy
    has = (
        (gx + n_gx - 1) // n_gx,
        1 - (gx + 1) // n_gx,
        (gy + n_gy - 1) // n_gy,
        1 - (gy + 1) // n_gy,
    )
    peers = ({"gx": gx - 1}, {"gx": gx + 1}, {"gy": gy - 1}, {"gy": gy + 1})
    combustor = sa == 0
    turbine = sa == 1
    at_exit = combustor & (gx == n_gx - 1)

    load_fields = pltpu.make_async_copy(fields.at[0], raw, local_sem.at[0])
    load_source = pltpu.make_async_copy(sources.at[0], raw_source, local_sem.at[1])
    load_diagonal = pltpu.make_async_copy(diagonal, raw_diagonal, local_sem.at[2])
    load_inverse = pltpu.make_async_copy(inverse, raw_inverse, local_sem.at[3])
    load_lists = pltpu.make_async_copy(donors, list_of, local_sem.at[4])
    load_returns = pltpu.make_async_copy(returns, returned, local_sem.at[5])
    load_weights = pltpu.make_async_copy(coupling, weights, local_sem.at[6])
    load_fields.start()
    pl.when(at_exit)(load_lists.start)
    pl.when(at_exit)(load_returns.start)
    load_source.start()
    pl.when(turbine)(load_weights.start)
    pl.when(combustor)(load_diagonal.start)
    pl.when(turbine)(load_inverse.start)

    barrier = pltpu.get_barrier_semaphore()

    def greet(peer):
        pl.semaphore_signal(barrier, inc=1, device_id=peer, device_id_type=MESH)

    for there, peer in zip(has, peers):
        pl.when(there == 1)(functools.partial(greet, peer))

    @pl.when(turbine)
    def _():
        for j in range(n_gy):
            greet({"gx": n_gx - 1, "gy": j, "sa": 0})

    @pl.when(at_exit)
    def _():
        for g in range(slots):
            greet({"gx": g // n_gy, "gy": g % n_gy, "sa": 1})

    sub = lax.broadcasted_iota(jnp.int32, (cells_y, LANES), 0)
    lane = lax.broadcasted_iota(jnp.int32, (cells_y, LANES), 1)
    tall = lax.broadcasted_iota(jnp.int32, (cells_y, cells_z), 0)
    wide = lax.broadcasted_iota(jnp.int32, (cells_y, cells_z), 1)
    parity = (tall + wide) % 2
    even = parity == 0
    even_lanes = (sub + lane) % 2 == 0

    def split(even_plane, odd_plane):
        return (jnp.where(even, even_plane, odd_plane), jnp.where(even, odd_plane, even_plane))

    def split_planes(block, k, p):
        return split(block[k, PLANES[p][0]], block[k, PLANES[p][1]])

    def pack_x(values, *choices):
        moved = [pltpu.roll(values[k], 1, 0) for k in range(packs, states)]
        moved += [values[k] for k in range(states - packs, packs)]
        return [
            [jnp.where(chosen, values[k], moved[k]) for k in range(packs)] for chosen in choices
        ]

    def stage(colour, p, tile, values):
        if p == 0:
            faces = pack_x(values, even_lanes == (colour == 0), even_lanes == (colour == 1))
            for way in range(2):
                for k in range(packs):
                    at = (tile // chunk_tiles, tile % chunk_tiles)
                    edge_x[way, colour, at[0], at[1], k] = faces[way][k]
        for k in range(states):
            edge_y[0, colour, p, tile, k] = values[k][0:1]
            edge_y[1, colour, p, tile, k] = values[k][cells_y - 1 : cells_y]

    def halo_copy(way, colour, half, piece):
        edges, halos = (edge_x, halo_x) if way < 2 else (edge_y, halo_y)
        return pltpu.make_async_remote_copy(
            src_ref=edges.at[way % 2, colour, piece],
            dst_ref=halos.at[1 - way % 2, half, piece],
            send_sem=send_sem.at[way, half, piece],
            recv_sem=recv_sem.at[way, half, piece],
            device_id=peers[way],
            device_id_type=MESH,
        )

    def send(ways, colour, half, piece):
        for way in ways:
            pl.when(has[way] == 1)(lambda way=way: halo_copy(way, colour, half, piece).start())

    def wait_sent(colour, half):
        for way in range(4):
            @pl.when(has[way] == 1)
            def _():
                for piece in range(CHUNKS if way < 2 else pairs):
                    halo_copy(way, colour, half, piece).wait_send()

    def wait_received(ways, colour, half, piece):
        for way in ways:
            pl.when(has[way] == 1)(
                lambda way=way: halo_copy(way ^ 1, colour, half, piece).wait_recv()
            )

    def inlet_copy(j):
        return pltpu.make_async_remote_copy(
            src_ref=inlet.at[0],
            dst_ref=table.at[own],
            send_sem=slot_sem.at[j],
            recv_sem=interface_sem.at[0],
            device_id={"gx": n_gx - 1, "gy": j, "sa": 0},
            device_id_type=MESH,
        )

    def row_copy(g):
        return pltpu.make_async_remote_copy(
            src_ref=rows.at[g],
            dst_ref=arrived.at[gy],
            send_sem=slot_sem.at[g],
            recv_sem=interface_sem.at[1],
            device_id={"gx": g // n_gy, "gy": g % n_gy, "sa": 1},
            device_id_type=MESH,
        )

    @pl.when(has[0] == 0)
    def _():
        halo_x[0, 0:2] = jnp.zeros((2,) + halo_x.shape[2:], jnp.float32)

    @pl.when((has[1] == 0) & turbine)
    def _():
        halo_x[1, 0:2] = jnp.zeros((2,) + halo_x.shape[2:], jnp.float32)

    for side in range(2):
        @pl.when(has[2 + side] == 0)
        def _():
            halo_y[side, 0:2] = jnp.zeros((2,) + halo_y.shape[2:], jnp.float32)

    load_fields.wait()
    for k in range(states):
        for p in range(pairs):
            held[0, p, k], held[1, p, k] = split_planes(raw, k, p)
    for tile in range(tiles):
        lanes = pl.ds(tile * LANES, LANES)
        for p in range(pairs):
            stage(1, p, tile, [held[1, p, k, :, lanes] for k in range(states)])

    @pl.when(turbine)
    def _():
        row = jnp.zeros((cells_y, LANES), jnp.float32)
        for x in range(cells_x):
            row = jnp.where(lane % BLK == x * cells_y + sub, raw[0, x, :, 0:1], row)
        inlet[0] = jnp.sum(row, axis=0, keepdims=True)

    @pl.when(at_exit)
    def _():
        load_lists.wait()
        slot_row = lax.broadcasted_iota(jnp.int32, (slots, LANES), 0)
        in_state = tall * per_row + wide // BLK

        def take(e, total):
            block = jnp.where(list_of[0, e] == gy, list_of[1, e], -1)
            found = jnp.zeros((cells_y, cells_z), jnp.float32)
            for k in range(states):
                here = in_state == block - k * (cells_y * per_row)
                found = jnp.where(here, raw[k, cells_x - 1], found)
            row = jnp.sum(found, axis=0, keepdims=True)
            row = sum(row[:, i * LANES : (i + 1) * LANES] for i in range(cells_z // LANES))
            return jnp.where(slot_row == list_of[2, e], row, total)

        total = lax.fori_loop(0, slots, take, jnp.zeros((slots, LANES), jnp.float32), unroll=4)
        for g in range(slots):
            rows[g] = total[g : g + 1]

    met = has[0] + has[1] + has[2] + has[3] + sa * n_gy + (1 - sa) * (1 - has[1]) * slots
    pl.semaphore_wait(barrier, met)

    @pl.when(at_exit)
    def _():
        for g in range(slots):
            row_copy(g).start()

    for chunk in range(CHUNKS):
        send(X_WAYS, 1, 0, chunk)
    for p in range(pairs):
        send(Y_WAYS, 1, 0, p)

    @pl.when(turbine)
    def _():
        for j in range(n_gy):
            inlet_copy(j).start()

    @pl.when(at_exit)
    def _():
        spread_from = lax.broadcasted_iota(jnp.int32, (LANES, cells_z), 0) % per_row
        spread_to = lax.broadcasted_iota(jnp.int32, (LANES, cells_z), 1) // BLK
        spread = jnp.where(spread_from == spread_to, 1.0, 0.0)
        load_returns.wait()
        for k in range(states):
            ids = returned[0:1, k * LANES : (k + 1) * LANES].astype(jnp.float32)
            ids = jnp.where(lane // per_row == sub, ids, 0.0)
            wanted[k] = jnp.dot(
                ids, spread, preferred_element_type=jnp.float32
            )

    load_source.wait()
    for k in range(states):
        for p in range(pairs):
            source[0, p, k], source[1, p, k] = split_planes(raw_source, k, p)

    @pl.when(combustor)
    def _():
        load_diagonal.wait()
        for k in range(states):
            for p in range(pairs):
                first, second = split_planes(raw_diagonal, k, p)
                scale[0, p, k] = 1.0 / (6.0 + first)
                scale[1, p, k] = 1.0 / (6.0 + second)

    @pl.when(turbine)
    def _():
        load_weights.wait()
        load_inverse.wait()

        def pack(s, carry):
            for t in range(states):
                for p in range(pairs):
                    first, second = split_planes(raw_inverse.at[s], t, p)
                    matrix[0, p, t, s] = first
                    matrix[1, p, t, s] = second
            return carry

        lax.fori_loop(0, states, pack, 0)

    def inner_terms(colour, section):
        other = 1 - colour
        for p in range(pairs):
            values = [held[other, p, k] for k in range(states)]
            lower = [pltpu.roll(value, 1, 1) for value in values]
            upper = [pltpu.roll(value, cells_z - 1, 1) for value in values]
            for k in range(states):
                if section == 0:
                    before = lower[k - 1] if k > 0 else 0.0
                    after = upper[k + 1] if k < states - 1 else 0.0
                else:
                    before = held[colour, p, k, :, 0:1] if k > 0 else 0.0
                    after = 0.0
                total = held[other, 1, k]
                if p == 1:
                    total += held[other, 0, k]
                total += jnp.where(wide == 0, before, lower[k])
                total += jnp.where(wide == cells_z - 1, after, upper[k])
                total += jnp.where(tall == 0, 0.0, pltpu.roll(values[k], 1, 0))
                total += jnp.where(tall == cells_y - 1, 0.0, pltpu.roll(values[k], cells_y - 1, 0))
                if section == 1:
                    total = weights[k] * total
                part[p, k] = source[colour, p, k] + total

    def halo_terms(colour, half, p, tile):
        at = (tile // chunk_tiles, tile % chunk_tiles)
        upward = even_lanes == (colour == 1)
        slot = [half * there + colour * (1 - there) for there in has]
        totals = []
        for k in range(states):
            below = halo_y[0, slot[2], p, tile, k]
            above = halo_y[1, slot[3], p, tile, k]
            totals.append(jnp.where(sub == 0, below, jnp.where(sub == cells_y - 1, above, 0.0)))
        for k in range(packs if p == 0 else 0):
            below = halo_x[0, slot[0], at[0], at[1], k]
            above = halo_x[1, slot[1], at[0], at[1], k]
            totals[k] += jnp.where(upward, above, below)
            if k + packs < states:
                totals[k + packs] += pltpu.roll(jnp.where(upward, below, above), cells_y - 1, 0)
        return totals

    def half_sweep(colour, half, section):
        other = 1 - colour
        inner_terms(colour, section)
        wait_received(X_WAYS, other, half, 0)
        wait_received(Y_WAYS, other, half, 0)
        if colour == 0 and section == 0:
            @pl.when((half == 0) & at_exit)
            def _():
                pltpu.make_async_copy(table, table, interface_sem.at[0]).wait()

                def lay(k, carry):
                    ids = wanted[k]
                    plane = jnp.zeros((cells_y, cells_z), jnp.float32)
                    for g in range(slots):
                        row = jnp.concatenate([table[g]] * (cells_z // LANES), axis=1)
                        plane = jnp.where(ids == float(g), row, plane)
                    wanted[k] = plane
                    return carry

                lax.fori_loop(0, states, lay, 0)
                for tile in range(tiles):
                    lanes = pl.ds(tile * LANES, LANES)
                    planes = [wanted[k, :, lanes] for k in range(states)]
                    for c in range(2):
                        for k, packed in enumerate(pack_x(planes, even_lanes == (c == 1))[0]):
                            halo_x[1, c, tile // chunk_tiles, tile % chunk_tiles, k] = packed

        if colour == 0 and section == 1:
            @pl.when(half == 0)
            def _():
                pltpu.make_async_copy(arrived, arrived, interface_sem.at[1]).wait()
                row = arrived[0]
                for j in range(1, n_gy):
                    row = row + arrived[j]
                columns = [
                    jnp.sum(
                        jnp.where(lane % BLK == x * cells_y + sub, row, 0.0), axis=1, keepdims=True
                    )
                    for x in range(cells_x)
                ]
                for p in range(pairs):
                    for c in range(2):
                        cell = jnp.where(sub % 2 == c, columns[PLANES[p][0]], columns[PLANES[p][1]])
                        inflow[c, p] = jnp.where(lane == 0, cell, 0.0)

        def update(p, tile):
            lanes = pl.ds(tile * LANES, LANES)
            totals = halo_terms(colour, half, p, tile)
            if section == 0:
                results = [
                    (part[p, k, :, lanes] + totals[k]) * scale[colour, p, k, :, lanes]
                    for k in range(states)
                ]
            else:
                if tile == 0:
                    totals[0] += inflow[colour, p]
                result = None
                for t in range(states):
                    driving = part[p, t, :, lanes] + weights[t] * totals[t]
                    term = matrix[colour, p, t, :, :, lanes] * driving
                    result = term if result is None else result + term
                results = [result[k] for k in range(states)]
            for k in range(states):
                held[colour, p, k, :, lanes] = results[k]
            stage(colour, p, tile, results)

        going_on = pl.when(half < halves - 1)
        for chunk in range(CHUNKS):
            if chunk > 0:
                wait_received(X_WAYS, other, half, chunk)
            for tile in range(chunk * chunk_tiles, (chunk + 1) * chunk_tiles):
                update(0, tile)
            going_on(functools.partial(send, X_WAYS, colour, half + 1, chunk))
        going_on(functools.partial(send, Y_WAYS, colour, half + 1, 0))
        wait_received(Y_WAYS, other, half, 1)
        for tile in range(tiles):
            update(1, tile)
        going_on(functools.partial(send, Y_WAYS, colour, half + 1, 1))

        wait_sent(other, half)

    for section in range(2):
        @pl.when(sa == section)
        def _():
            def sweep(index, carry):
                half_sweep(0, 2 * index, section)
                half_sweep(1, 2 * index + 1, section)
                return carry

            lax.fori_loop(0, SWEEPS, sweep, 0)

    for k in range(states):
        for p in range(pairs):
            first, second = split(held[0, p, k], held[1, p, k])
            out[0, k, PLANES[p][0]] = first
            out[0, k, PLANES[p][1]] = second

    @pl.when(turbine)
    def _():
        for j in range(n_gy):
            inlet_copy(j).wait_send()

    @pl.when(at_exit)
    def _():
        for g in range(slots):
            row_copy(g).wait_send()


def shards(n_gx, n_gy, fields, sources, diagonal, block_inverse, coupling, donors, returns):
    _, states, cells_x, cells_y, cells_z = fields.shape
    pairs = len(PLANES)
    slots = donors.shape[0]
    assert cells_x == 4 and cells_y % 2 == 0 and cells_x * cells_y == BLK
    assert cells_y * cells_z == LANES * BLK and slots == n_gx * n_gy
    f32 = jnp.float32
    block = (states, cells_x, cells_y, cells_z)
    halves = 2 * SWEEPS
    tiles = cells_z // LANES
    packs = (states + 1) // 2
    chunk = (CHUNKS, tiles // CHUNKS)
    operands = [
        pltpu.with_memory_space_constraint(operand, pltpu.HBM)
        for operand in (fields, sources, diagonal, block_inverse, coupling, donors.T, returns)
    ]
    hbm = pl.BlockSpec(memory_space=pltpu.HBM)
    vmem = pl.BlockSpec(memory_space=pltpu.VMEM)
    by_colour = (2, pairs, states, cells_y, cells_z)
    return pl.pallas_call(
        functools.partial(kernel, n_gx, n_gy, block),
        out_shape=jax.ShapeDtypeStruct(fields.shape, f32),
        in_specs=[hbm] * 7,
        out_specs=vmem,
        scratch_shapes=[
            pltpu.VMEM(block, f32),
            pltpu.VMEM(block, f32),
            pltpu.VMEM(block, f32),
            pltpu.VMEM((states,) + block, f32),
            pltpu.SMEM(coupling.shape, f32),
            pltpu.SMEM(donors.shape[::-1], jnp.int32),
            pltpu.VMEM(returns.shape, jnp.int32),
            pltpu.VMEM(by_colour, f32),
            pltpu.VMEM(by_colour, f32),
            pltpu.VMEM(by_colour, f32),
            pltpu.VMEM((2, pairs, states, states, cells_y, cells_z), f32),
            pltpu.VMEM(by_colour[1:], f32),
            pltpu.VMEM((2, halves) + chunk + (packs, cells_y, LANES), f32),
            pltpu.VMEM((2, halves, pairs, tiles, states, 1, LANES), f32),
            pltpu.VMEM((2, 2) + chunk + (packs, cells_y, LANES), f32),
            pltpu.VMEM((2, 2, pairs, tiles, states, 1, LANES), f32),
            pltpu.VMEM((2, pairs, cells_y, LANES), f32),
            pltpu.VMEM((states, cells_y, cells_z), f32),
            pltpu.VMEM((slots, 1, LANES), f32),
            pltpu.VMEM((slots, 1, LANES), f32),
            pltpu.VMEM((1, 1, LANES), f32),
            pltpu.VMEM((n_gy, 1, LANES), f32),
            pltpu.SemaphoreType.DMA((7,)),
            pltpu.SemaphoreType.DMA((4, halves, max(CHUNKS, pairs))),
            pltpu.SemaphoreType.DMA((4, halves, max(CHUNKS, pairs))),
            pltpu.SemaphoreType.DMA((slots,)),
            pltpu.SemaphoreType.DMA((2,)),
        ],
        compiler_params=pltpu.CompilerParams(
            collective_id=0, has_side_effects=True, vmem_limit_bytes=32 * 1024 * 1024
        ),
    )(*operands)


def solution(mesh):
    return jax.shard_map(
        functools.partial(shards, mesh.shape["gx"], mesh.shape["gy"]),
        mesh=mesh,
        in_specs=(
            P("sa", None, "gx", "gy", None),
            P("sa", None, "gx", "gy", None),
            P(None, "gx", "gy", None),
            P(None, None, "gx", "gy", None),
            P(),
            P(),
            P("gy", None),
        ),
        out_specs=P("sa", None, "gx", "gy", None),
        check_vma=False,
    )
```
